128 devices in a mesh: sec: 4 (over z), space: 32 (over x, y, core).
Axes of the slice: x: 4, y: 4, z: 4, core: 2. Of those that a mesh axis runs over, the one named last changes fastest.
Arguments:
- grid_feat: bfloat16 [4, 32768, 1024], P('sec', 'space'), may hold values from -12 to 12
- mesh_feat: bfloat16 [4, 16384, 1024], P('sec', 'space'), may hold values from -27 to 27
- mesh_adjoint: bfloat16 [4, 16384, 1024], P('sec', 'space'), may hold values from -6 to 6
- w_query: bfloat16 [1024, 1024], replicated, may hold values from -1 to 1
- w_key: bfloat16 [1024, 1024], replicated, may hold values from -1 to 1
- w_value: bfloat16 [1024, 1024], replicated, may hold values from -0.1875 to 0.1875
- block_grid: int32 [512], P('space'), may hold values from 0 to 255, as said below
- block_mask: int32 [512, 128, 128], P('space'), may hold values from 0 to 1, as said below
Outputs:
- grid_grad: bfloat16 [4, 32768, 1024], P('sec', 'space')
- mesh_grad: bfloat16 [4, 16384, 1024], P('sec', 'space')
- w_grad: float32 [1024, 3072], P(('sec', 'space'))
The draws below stay inside these ranges and needn't reach their ends.
Inputs may be any that keep to these rules, and one draw needn't show every extreme that they name: `block_grid`: each mesh block of a band has 4 consecutive slots listing distinct grid blocks of its own band or the nearest block of an adjacent band; the first is the own band's block number m * 2 within the band for mesh block m; where the band below exists, the band's first mesh block lists its nearest block in the second slot; where the band above exists, the band's last mesh block lists its nearest block in the second slot. `block_mask`: the first slot of each mesh block holds the diagonal, so every mesh node has an edge; in each band, the last slots of every mesh block (the same number for all of its mesh blocks, at least min(3, 4) slots live) may be all zeros; band 0 has none such.
All inputs are finite; a program needn't handle non-finite values.
Results may differ from the reference program's by a relative error of at most 0.015.
The reference program's roundings to bfloat16 on the way count: a program that leaves them out, or rounds other values in their place, can miss the bound.
Values may be sent and summed in bfloat16 or wider, within the bound.
A program may use at most 128 MiB of HBM per device.

```python
import jax
import jax.numpy as jnp
from jax import lax

D = 1024
DH = 64
BLOCK = 128
K = 4
G_DEV = 1024
M_DEV = 512
GRID = 32768
NODES = 16384
N_SEC = 4
N_SPACE = 32


def grid_base(key):
    inner = jax.random.fold_in(key, 11)
    return jnp.clip(jax.random.normal(inner, (N_SEC, GRID, D), jnp.float32), -6.0, 6.0)


def weight_base(key):
    inner = jax.random.fold_in(key, 21)
    return jnp.clip(jax.random.normal(inner, (D, D), jnp.float32), -4.0, 4.0) / D ** 0.5


def draw_grid_feat(key, part):
    base = grid_base(key)
    return base.astype(jnp.bfloat16)


def draw_mesh_feat(key, part):
    key = jax.random.fold_in(key, 2)
    own = jnp.clip(jax.random.normal(key, (N_SEC, NODES, D), jnp.float32), -6.0, 6.0)
    return own.astype(jnp.bfloat16)


def draw_w_query(key, part):
    base = weight_base(key)
    return base.astype(jnp.bfloat16)


def draw_w_key(key, part):
    key = jax.random.fold_in(key, 4)
    own = jnp.clip(jax.random.normal(key, (D, D), jnp.float32), -4.0, 4.0) / D ** 0.5
    return own.astype(jnp.bfloat16)


def graph_lists(key):
    inner = jax.random.fold_in(key, 31)
    grid_blocks = G_DEV // BLOCK
    mesh_blocks = M_DEV // BLOCK
    cand = jnp.arange(grid_blocks + 2, dtype=jnp.int32)
    band = jnp.arange(N_SPACE, dtype=jnp.int32)
    globe = band[:, None] * grid_blocks - 1 + cand[None, :]
    valid = (globe >= 0) & (globe < N_SPACE * grid_blocks)
    mesh_idx = jnp.arange(mesh_blocks, dtype=jnp.int32)
    forced = 1 + mesh_idx * grid_blocks // mesh_blocks
    scores = jax.random.randint(inner, (N_SPACE, mesh_blocks, grid_blocks + 2), 0, 2 ** 20) * 16 + cand
    low_rim = (cand[None, :] == 0) & (mesh_idx[:, None] == 0)
    high_rim = (cand[None, :] == grid_blocks + 1) & (mesh_idx[:, None] == mesh_blocks - 1)
    scores = jnp.where(low_rim[None], 2 ** 25, scores)
    scores = jnp.where(high_rim[None], 2 ** 24, scores)
    scores = jnp.where(valid[:, None, :], scores, -1)
    scores = jnp.where(cand[None, None, :] == forced[None, :, None], 2 ** 26, scores)
    chosen = jax.lax.top_k(scores, K)[1].astype(jnp.int32)
    ids = band[:, None, None] * grid_blocks - 1 + chosen
    return ids.reshape(N_SPACE * mesh_blocks * K)


def draw_block_grid(key, part):
    ids = graph_lists(key)
    return ids


def draw_block_mask(key, part):
    key = jax.random.fold_in(key, 6)
    mesh_blocks = M_DEV // BLOCK
    first, second = jax.random.split(key)
    live_count = jax.random.randint(first, (N_SPACE,), min(3, K), K + 1)
    live_count = jnp.where(jnp.arange(N_SPACE) == 0, K, live_count)
    slot = jnp.arange(K, dtype=jnp.int32)
    live = slot[None, :] < live_count[:, None]
    bits = jax.random.randint(second, (N_SPACE, mesh_blocks, K, BLOCK, BLOCK), 0, 4) == 0
    diag = jnp.eye(BLOCK, dtype=jnp.int32) > 0
    with_diag = bits | (slot == 0)[None, None, :, None, None] & diag[None, None, None]
    mask = with_diag & live[:, None, :, None, None]
    return mask.astype(jnp.int32).reshape(N_SPACE * mesh_blocks * K, BLOCK, BLOCK)


def block_scale(rng, shape, pieces, least, largest):
    def one(axis_at, parts):
        heights = jax.random.uniform(jax.random.fold_in(jax.random.fold_in(rng, 6), axis_at), (parts,), jnp.float32, least / len(pieces), largest / len(pieces))
        return jnp.repeat(jnp.exp(heights), shape[axis_at] // parts).reshape((-1,) + (1,) * (len(shape) - axis_at - 1))

    gain = one(*pieces[0])
    for cut in pieces[1:]:
        gain = gain * one(*cut)
    return gain


def scatter_about(key, shape, scale, most, cuts=(), kind=jnp.bfloat16):
    entries = jax.random.normal(key, shape, jnp.float32) * scale
    if len(cuts) > 0:
        entries = block_scale(key, shape, cuts, -0.22, 0.18) * entries
    return jnp.clip(entries, min=-most, max=most).astype(kind)


def setup_inputs(seed: int = 0) -> dict:
    seeds = jax.random.split(jax.random.key(seed), 9)
    return {
        "grid_feat": draw_grid_feat(jax.random.fold_in(seeds[8], 71), 0),
        "mesh_feat": draw_mesh_feat(jax.random.fold_in(seeds[8], 71), 0),
        "mesh_adjoint": scatter_about(seeds[2], (N_SEC, NODES, D), 1.0, 6.0, ((0, 4), (1, 32))),
        "w_query": draw_w_query(jax.random.fold_in(seeds[8], 71), 0),
        "w_key": draw_w_key(jax.random.fold_in(seeds[8], 71), 0),
        "w_value": scatter_about(seeds[5], (D, D), D ** -0.5, 0.1875),
        "block_grid": draw_block_grid(jax.random.fold_in(seeds[8], 71), 0),
        "block_mask": draw_block_mask(jax.random.fold_in(seeds[8], 71), 0),
    }


def times_transposed(left, weight):
    return lax.dot_general(left, weight, (((1,), (1,)), ((), ())), preferred_element_type=jnp.float32)


def attend(query_blk, adjoint_blk, kv_rows, masks):
    rows = query_blk.shape[0]
    width = query_blk.shape[1]
    heads = width // DH
    scale = DH ** -0.5
    query_h = query_blk.reshape(rows, heads, DH).astype(jnp.float32)
    keys = kv_rows[:, :width].reshape(-1, heads, DH)
    values = kv_rows[:, width:].reshape(-1, heads, DH)
    live = masks.transpose(1, 0, 2).reshape(rows, -1) > 0
    scores = jnp.einsum("rhd,chd->hrc", query_h, keys.astype(jnp.float32)) * scale
    shifted = jnp.where(live[None], scores, -1e30)
    top = jnp.max(shifted, axis=-1, keepdims=True)
    expo = jnp.where(live[None], jnp.exp(shifted - top), 0.0)
    probs = expo / jnp.sum(expo, axis=-1, keepdims=True)
    probs_b = probs.astype(jnp.bfloat16)
    attended = jnp.einsum("hrc,chd->rhd", probs_b.astype(jnp.float32), values.astype(jnp.float32))
    adjoint_h = adjoint_blk.reshape(rows, heads, DH).astype(jnp.float32)
    delta = jnp.sum(adjoint_h * attended, axis=-1).T[:, :, None]
    dprobs = jnp.einsum("rhd,chd->hrc", adjoint_h, values.astype(jnp.float32))
    dscores = (probs * (dprobs - delta) * scale).astype(jnp.bfloat16).astype(jnp.float32)
    dquery = jnp.einsum("hrc,chd->rhd", dscores, keys.astype(jnp.float32)).reshape(rows, width)
    dkey = jnp.einsum("hrc,rhd->chd", dscores, query_h).reshape(-1, width)
    dvalue = jnp.einsum("hrc,rhd->chd", probs_b.astype(jnp.float32), adjoint_h).reshape(-1, width)
    return dquery, jnp.concatenate([dkey, dvalue], axis=1)


def reference(grid_feat, mesh_feat, mesh_adjoint, w_query, w_key, w_value, block_grid, block_mask):
    mesh_blocks = M_DEV // BLOCK
    w_both = jnp.concatenate([w_key, w_value], axis=1)
    weight_total = jnp.zeros((D, 3 * D), jnp.float32)
    grid_out = []
    mesh_out = []
    for sample in range(N_SEC):
        feats = grid_feat[sample]
        nodes = mesh_feat[sample]
        arrived = mesh_adjoint[(sample + 1) % N_SEC]
        queries = jnp.dot(nodes, w_query, preferred_element_type=jnp.float32).astype(jnp.bfloat16)
        kv_all = jnp.dot(feats, w_both, preferred_element_type=jnp.float32).astype(jnp.bfloat16)
        kv_blocks = kv_all.reshape(GRID // BLOCK, BLOCK, 2 * D)

        def step(acc, index):
            start = (index * K).astype(jnp.int32)
            ids = lax.dynamic_slice_in_dim(block_grid, start, K)
            masks = lax.dynamic_slice_in_dim(block_mask, start, K, 0)
            query_blk = lax.dynamic_slice_in_dim(queries, (index * BLOCK).astype(jnp.int32), BLOCK, 0)
            adjoint_blk = lax.dynamic_slice_in_dim(arrived, (index * BLOCK).astype(jnp.int32), BLOCK, 0)
            kv_rows = kv_blocks[ids].reshape(K * BLOCK, 2 * D)
            dquery, dkv = attend(query_blk, adjoint_blk, kv_rows, masks)
            acc = acc.at[ids].add(dkv.reshape(K, BLOCK, 2 * D))
            return acc, dquery

        start_acc = jnp.zeros((GRID // BLOCK, BLOCK, 2 * D), jnp.float32)
        acc, dqueries = lax.scan(step, start_acc, jnp.arange(N_SPACE * mesh_blocks, dtype=jnp.int32))
        dquery_b = dqueries.reshape(NODES, D).astype(jnp.bfloat16)
        dkv_b = acc.reshape(GRID, 2 * D).astype(jnp.bfloat16)
        grid_grad = (times_transposed(dkv_b[:, :D], w_key) + times_transposed(dkv_b[:, D:], w_value)).astype(jnp.bfloat16)
        mesh_grad = times_transposed(dquery_b, w_query).astype(jnp.bfloat16)
        mesh_term = lax.dot_general(nodes, dquery_b, (((0,), (0,)), ((), ())), preferred_element_type=jnp.float32)
        grid_term = lax.dot_general(feats, dkv_b, (((0,), (0,)), ((), ())), preferred_element_type=jnp.float32)
        weight_total = weight_total + jnp.concatenate([mesh_term, grid_term], axis=1)
        grid_out.append(grid_grad)
        mesh_out.append(mesh_grad)
    return jnp.stack(grid_out), jnp.stack(mesh_out), weight_total / N_SEC
```

```python
import jax
import jax.numpy as jnp
from jax import lax
from jax.experimental import pallas as pl
from jax.experimental.pallas import tpu as pltpu
from jax.sharding import PartitionSpec as P

LOG2E = 1.4426950408889634
F32, BF16 = jnp.float32, jnp.bfloat16

def nt(a, b):
    return lax.dot_general(a, b, (((1,), (1,)), ((), ())), preferred_element_type=F32)
def tn(a, b):
    return lax.dot_general(a, b, (((0,), (0,)), ((), ())), preferred_element_type=F32)
def nn(a, b):
    return lax.dot_general(a, b, (((1,), (0,)), ((), ())), preferred_element_type=F32)

def paired(x):
    left = lax.broadcasted_iota(jnp.int32, x.shape, 1) < 64
    zero = jnp.zeros_like(x)
    return jnp.concatenate([jnp.where(left, x, zero), jnp.where(left, zero, x)], axis=0)

def attend(ids_ref, m, cols, q_ref, a_ref, k_ref, v_ref, bias_ref, dq_ref, dk_part, dv_part):
    rows = pl.ds(m * 128, 128)
    starts = [pl.multiple_of(ids_ref[m * 4 + s] * 128, 128) for s in range(4)]
    keys = jnp.concatenate([k_ref[pl.ds(b, 128), cols] for b in starts], axis=0)
    values = jnp.concatenate([v_ref[pl.ds(b, 128), cols] for b in starts], axis=0)
    qq = paired(q_ref[rows, cols] * 0.125)
    aa = paired(a_ref[rows, cols])
    bias = bias_ref[m]
    bias = jnp.concatenate([bias, bias], axis=1)
    scores = nt(keys, qq) + bias
    top = jnp.max(scores, axis=0, keepdims=True)
    expo = jnp.exp2((scores - top) * LOG2E)
    probs = expo * (1.0 / jnp.sum(expo, axis=0, keepdims=True))
    probs_b = probs.astype(BF16)
    dprobs = nt(values, aa)
    delta = jnp.sum(probs_b.astype(F32) * dprobs, axis=0, keepdims=True)
    ds = (probs * (dprobs - delta)).astype(BF16)
    dv = nn(probs_b, aa)
    dk = nn(ds, qq)
    for s in range(4):
        dv_part[m * 4 + s] = dv[s * 128:(s + 1) * 128]
        dk_part[m * 4 + s] = dk[s * 128:(s + 1) * 128]
    dq = tn(keys, ds)
    dq = jnp.concatenate([dq[:64, :128], dq[64:, 128:]], axis=0) * 0.125
    dq_ref[rows, cols] = dq.T.astype(BF16)

def kernel(ids_ref, q_ref, a_ref, k_ref, v_ref, mask_ref, dq_ref, dk_ref, dv_ref, bias_ref, dk_part, dv_part):
    for e in range(16):
        bias_ref[e // 4, (e % 4) * 128:(e % 4 + 1) * 128, :] = (mask_ref[e].astype(F32).T - 1.0) * 1e30
    dk_part[16] = jnp.zeros((128, 128), F32)
    dv_part[16] = jnp.zeros((128, 128), F32)

    @pl.loop(0, 8)
    def _(pair):
        cols = pl.ds(pl.multiple_of(pair * 128, 128), 128)
        for m in range(4):
            attend(ids_ref, m, cols, q_ref, a_ref, k_ref, v_ref, bias_ref, dq_ref, dk_part, dv_part)

        @pl.loop(0, 10)
        def _(block):
            at = []
            for m in range(4):
                where = 16
                for s in range(4):
                    where = jnp.where(ids_ref[m * 4 + s] == block, m * 4 + s, where)
                at.append(where)
            rows = pl.ds(pl.multiple_of(block * 128, 128), 128)
            dk_ref[rows, cols] = ((dk_part[at[0]] + dk_part[at[1]]) + (dk_part[at[2]] + dk_part[at[3]])).astype(dk_ref.dtype)
            dv_ref[rows, cols] = ((dv_part[at[0]] + dv_part[at[1]]) + (dv_part[at[2]] + dv_part[at[3]])).astype(dv_ref.dtype)

def call(ids, q, a, k, v, mask):
    vm = pl.BlockSpec(memory_space=pltpu.VMEM)
    return pl.pallas_call(
        kernel,
        in_specs=[pl.BlockSpec(memory_space=pltpu.SMEM)] + [vm] * 5,
        out_specs=[vm] * 3,
        out_shape=[jax.ShapeDtypeStruct((512, 1024), BF16), jax.ShapeDtypeStruct((1280, 1024), F32), jax.ShapeDtypeStruct((1280, 1024), F32)],
        scratch_shapes=[pltpu.VMEM((4, 512, 128), F32), pltpu.VMEM((17, 128, 128), F32), pltpu.VMEM((17, 128, 128), F32)],
        compiler_params=pltpu.CompilerParams(vmem_limit_bytes=60 << 20),
    )(ids, q, a, k, v, mask)

def passed_along(value, axis, steps):
    count = lax.axis_size(axis)
    pairs = [(source, (source + steps) % count) for source in range(count)]
    return lax.ppermute(value, axis, pairs)


def with_halo(shard, sides, width):
    for axis, dim in sides:
        devices, length = (lax.axis_size(axis), shard.shape[dim])
        up = [(i, (i + 1) % devices) for i in range(devices - 1)]
        down = [(j, i) for i, j in up]
        last = lax.slice_in_dim(shard, length - width, length, axis=dim)
        initial = lax.slice_in_dim(shard, 0, width, axis=dim)
        before = lax.ppermute(last, axis, up)
        after = lax.ppermute(initial, axis, down)
        shard = jnp.concatenate([before, shard, after], axis=dim)
    return shard


def passed_along_2(shard, axis, by):
    devices = lax.axis_size(axis)
    pairs = [(i, i + by) for i in range(devices) if 0 <= i + by < devices]
    return lax.ppermute(shard, axis, pairs)


def times_transposed(left, weight):
    return lax.dot_general(
        left, weight, (((1,), (1,)), ((), ())), preferred_element_type=jnp.float32
    )


def on_device(grid_feat, mesh_feat, mesh_adjoint, w_query, w_key, w_value, block_grid, block_mask):
    arrived = passed_along(mesh_adjoint, "sec", -1)[0]
    feats = grid_feat[0]
    nodes = mesh_feat[0]
    band = lax.axis_index("space")
    own_k = nn(feats, w_key).astype(BF16)
    own_v = nn(feats, w_value).astype(BF16)
    keys = with_halo(own_k, (("space", 0),), 128)
    values = with_halo(own_v, (("space", 0),), 128)
    queries = nn(nodes, w_query).astype(BF16)
    local_ids = block_grid - band * 8 + 1
    dquery, dkey, dvalue = call(local_ids, queries, arrived, keys, values, block_mask)

    def folded(acc):
        above = passed_along_2(acc[:128].astype(BF16), "space", -1).astype(F32)
        below = passed_along_2(acc[-128:].astype(BF16), "space", 1).astype(F32)
        core = acc[128:-128]
        core = core.at[-128:].add(above)
        core = core.at[:128].add(below)
        return core.astype(BF16)

    dkey = folded(dkey)
    dvalue = folded(dvalue)
    grid_grad = (times_transposed(dkey, w_key) + times_transposed(dvalue, w_value)).astype(BF16)
    mesh_grad = times_transposed(dquery, w_query).astype(BF16)
    terms = jnp.concatenate([tn(nodes, dquery), tn(feats, dkey), tn(feats, dvalue)], axis=1) * 0.25
    w_grad = lax.psum_scatter(terms.astype(BF16), ("sec", "space"), scatter_dimension=0, tiled=True)
    return (grid_grad[None], mesh_grad[None], w_grad.astype(F32))


def solution(mesh):
    placed = (
        P("sec", "space", None),
        P("sec", "space", None),
        P("sec", "space", None),
        P(),
        P(),
        P(),
        P("space"),
        P("space", None, None),
    )
    return jax.shard_map(
        on_device,
        mesh=mesh,
        in_specs=placed,
        out_specs=(P("sec", "space", None), P("sec", "space", None), P(("sec", "space"), None)),
        check_vma=False,
    )
```

```python
import jax
import jax.numpy as jnp
from jax import lax
from jax.experimental import pallas as pl
from jax.experimental.pallas import tpu as pltpu
from jax.sharding import PartitionSpec as P

F32, BF16 = jnp.float32, jnp.bfloat16
MESH = pl.DeviceIdType.MESH
D = 1024
GROUPS = 4
W = D // GROUPS
PAIRS = W // 128
BANDS = 32
ORDERS = ((0, 1, 2), (1, 2, 0), (2, 0, 1))


def nt(a, b):
    return lax.dot_general(a, b, (((1,), (1,)), ((), ())), preferred_element_type=F32)


def tn(a, b):
    return lax.dot_general(a, b, (((0,), (0,)), ((), ())), preferred_element_type=F32)


def nn(a, b):
    return lax.dot_general(a, b, (((1,), (0,)), ((), ())), preferred_element_type=F32)


def paired(x):
    left = lax.broadcasted_iota(jnp.int32, x.shape, 1) < 64
    zero = jnp.zeros_like(x)
    return jnp.concatenate([jnp.where(left, x, zero), jnp.where(left, zero, x)], axis=0)


def kernel(
    ids_ref, x_hbm, h_hbm, a_hbm, wq_hbm, wk_hbm, wv_hbm, mask_hbm,
    gg_hbm, mg_hbm, wg_hbm,
    x_ref, h_ref, xt_ref, ht_ref, w_ref, mask_ref, bias_ref, adj_ref, q_ref, k_ref, v_ref,
    dq_ref, dk_ref, dv_ref, dk_part, dv_part, edge_ref,
    kv_out, kv_in, dkv_out, dkv_in,
    term_ref, core_in, a_out, a_in, b_out, b_in, c_out, c_in, wg_ref, gg_ref, mg_ref,
    local_ref, lists_ref, load_sem, w_sem, out_sem, adj_sem, kv_sem, dkv_sem, core_sem, a_sem, b_sem, c_sem,
):
    sec = lax.axis_index("sec")
    band = lax.axis_index("space")
    core = band % 2
    gx = band // 8
    gy = (band // 2) % 4
    place = (sec, gx, gy)

    def space_of(x, y, c):
        return (x * 4 + y) * 2 + c

    def peer(axis, steps):
        z, x, y = place
        if axis == 0:
            return ((z + steps) % 4, band)
        if axis == 1:
            return (z, space_of((x + steps) % 4, y, core))
        return (z, space_of(x, (y + steps) % 4, core))

    sibling = (sec, space_of(gx, gy, 1 - core))
    up = (sec, (band + 1) % BANDS)
    down = (sec, (band + BANDS - 1) % BANDS)
    across = (sec, (band + BANDS + 2 * core - 1) % BANDS)

    def cols_of(g):
        return pl.ds(pl.multiple_of(g * W, W), W)

    def load(src, dst, i):
        return pltpu.make_async_copy(src, dst, load_sem.at[i])

    def load_w(g, i):
        return pltpu.make_async_copy(
            (wq_hbm, wk_hbm, wv_hbm)[i].at[:, cols_of(g)], w_ref.at[i, :, cols_of(g)], w_sem.at[g, i]
        )

    def remote(src, dst, sem, at, to):
        return pltpu.make_async_remote_copy(
            src_ref=src, dst_ref=dst, send_sem=sem.at[(0, *at)], recv_sem=sem.at[(1, *at)],
            device_id=to, device_id_type=MESH,
        )

    barrier = pltpu.get_barrier_semaphore()
    peers = [sibling, across] + [peer(axis, steps) for axis in range(3) for steps in (1, 2, 3)]
    for to in peers:
        pl.semaphore_signal(barrier, inc=1, device_id=to, device_id_type=MESH)
    load(x_hbm, x_ref, 0).start()
    for i in (1, 2):
        load_w(0, i).start()
    load(h_hbm, h_ref, 1).start()
    load_w(0, 0).start()
    load(mask_hbm, mask_ref, 2).start()
    for g in range(1, GROUPS):
        for i in range(3):
            load_w(g, i).start()
    pl.semaphore_wait(barrier, len(peers))

    def adjoint(g):
        return remote(a_hbm.at[:, cols_of(g)], adj_ref.at[g], adj_sem, (g,), peer(0, 3))

    for g in range(GROUPS):
        adjoint(g).start()

    def halo(g, side):
        return remote(kv_out.at[g, side], kv_in.at[g, 1 - side], kv_sem, (g, side), (down, up)[side])

    def project(g):
        turn = g % 2
        for i in (1, 2):
            load_w(g, i).wait()
            own = nn(x_ref[...], w_ref[i, :, cols_of(g)]).astype(BF16)
            for b in range(8):
                (k_ref, v_ref)[i - 1][turn, b + 1] = own[b * 128:(b + 1) * 128]
            kv_out[g, 0, i - 1] = own[:128]
            kv_out[g, 1, i - 1] = own[896:]
        for side in range(2):
            halo(g, side).start()
        load_w(g, 0).wait()
        q_ref[turn] = (nn(h_ref[...], w_ref[0, :, cols_of(g)]).astype(BF16)) * 0.125

    load(x_hbm, x_ref, 0).wait()
    load(h_hbm, h_ref, 1).wait()
    project(0)

    @pl.loop(0, 8)
    def _(i):
        rows = pl.ds(pl.multiple_of(i * 128, 128), 128)
        xt_ref[:, rows] = x_ref[rows, :].T

    @pl.loop(0, 4)
    def _(i):
        rows = pl.ds(pl.multiple_of(i * 128, 128), 128)
        ht_ref[:, rows] = h_ref[rows, :].T

    load(mask_hbm, mask_ref, 2).wait()

    @pl.loop(0, 4)
    def _(m):
        for s in range(4):
            bias_ref[m, s * 128:(s + 1) * 128, :] = (mask_ref[m * 4 + s].astype(F32).T - 1.0) * 1e30

    dk_part[16] = jnp.zeros((128, 128), F32)
    dv_part[16] = jnp.zeros((128, 128), F32)

    for e in range(16):
        local_ref[e] = jnp.clip(ids_ref[e] - band * 8 + 1, 0, 9)
    for block in range(10):
        for m in range(4):
            at = 16
            for s in range(4):
                off = local_ref[m * 4 + s] - block
                at = at + (1 - jnp.minimum(off * off, 1)) * (m * 4 + s - 16)
            lists_ref[block * 4 + m] = jnp.clip(at, 0, 16)

    def attend(g, pair, m):
        turn = g % 2
        rows = slice(m * 128, (m + 1) * 128)
        cols = pl.ds(pl.multiple_of(pair * 128, 128), 128)
        blocks = [local_ref[m * 4 + s] for s in range(4)]
        keys = jnp.concatenate([k_ref[turn, b, :, cols] for b in blocks], axis=0)
        values = jnp.concatenate([v_ref[turn, b, :, cols] for b in blocks], axis=0)
        qq = paired(q_ref[turn, rows, cols])
        aa = paired(adj_ref[g, rows, cols])
        bias = bias_ref[m]
        bias = jnp.concatenate([bias, bias], axis=1)
        scores = nt(keys, qq) + bias
        top = jnp.max(scores, axis=0, keepdims=True)
        expo = jnp.exp(scores - top)
        probs = expo * (1.0 / jnp.sum(expo, axis=0, keepdims=True))
        probs_b = probs.astype(BF16)
        dprobs = nt(values, aa)
        delta = jnp.sum(probs_b.astype(F32) * dprobs, axis=0, keepdims=True)
        ds = (probs * (dprobs - delta)).astype(BF16)
        dv = nn(probs_b, aa)
        dk = nn(ds, qq)
        for s in range(4):
            dv_part[m * 4 + s] = dv[s * 128:(s + 1) * 128]
            dk_part[m * 4 + s] = dk[s * 128:(s + 1) * 128]
        dq = tn(keys, ds)
        dq = jnp.concatenate([dq[:64, :128], dq[64:, 128:]], axis=0) * 0.125
        dq_ref[g, rows, cols] = dq.T.astype(BF16)

    def gathered(part, block):
        found = [part[lists_ref[block * 4 + m]] for m in range(4)]
        return (found[0] + found[1]) + (found[2] + found[3])

    def attend_pair(g, pair):
        cols = pl.ds(pl.multiple_of(pair * 128, 128), 128)
        for m in range(4):
            attend(g, pair, m)
        for i, part in enumerate((dk_part, dv_part)):
            dkv_out[g, 0, i, :, cols] = gathered(part, 0).astype(BF16)
            dkv_out[g, 1, i, :, cols] = gathered(part, 9).astype(BF16)
            edge_ref[g % 2, 0, i, :, cols] = gathered(part, 1)
            edge_ref[g % 2, 1, i, :, cols] = gathered(part, 8)

        @pl.loop(1, 7)
        def _(block):
            rows = pl.ds(pl.multiple_of(block * 128, 128), 128)
            dk_ref[g, rows, cols] = gathered(dk_part, block + 1).astype(BF16)
            dv_ref[g, rows, cols] = gathered(dv_part, block + 1).astype(BF16)

    def back(g, side):
        return remote(dkv_out.at[g, side], dkv_in.at[g, 1 - side], dkv_sem, (g, side), (down, up)[side])

    def merge(g):
        for side in range(2):
            back(g, side).wait()
        for i, ref in enumerate((dk_ref, dv_ref)):
            ref[g, 0:128, :] = (edge_ref[g % 2, 0, i] + dkv_in[g, 0, i].astype(F32)).astype(BF16)
            ref[g, 896:1024, :] = (edge_ref[g % 2, 1, i] + dkv_in[g, 1, i].astype(F32)).astype(BF16)

    def swap(g):
        return remote(term_ref.at[g, 1 - core], core_in.at[g], core_sem, (g,), sibling)

    def terms(g):
        for t in range(3):
            if t == 0:
                term = nn(ht_ref[...], dq_ref[g])
            else:
                term = nn(xt_ref[...], (dk_ref, dv_ref)[t - 1][g])
            strides = [(256, 64, 16)[axis] for axis in ORDERS[t]]
            for c in range(2):
                for j in range(0, 64, 2):
                    pieces = []
                    for n in (j, j + 1):
                        row = (n // 16) * strides[0] + (n // 4 % 4) * strides[1] + (n % 4) * strides[2] + c * 8
                        pieces.append(term[row:row + 8])
                    term_ref[g, c, t, j * 8:j * 8 + 16, :] = jnp.concatenate(pieces, axis=0).astype(BF16)
        swap(g).start()

    stages = ((a_out, a_in, a_sem, 128), (b_out, b_in, b_sem, 32), (c_out, c_in, c_sem, 8))

    def pass_on(g, level, t, steps):
        out, inside, sem, rows = stages[level]
        axis = ORDERS[t][level]
        first = pl.multiple_of((place[axis] + steps) % 4 * rows, rows)
        return remote(
            out.at[g, t, pl.ds(first, rows), :], inside.at[g, t, steps - 1], sem, (g, t, steps - 1), peer(axis, steps)
        )

    def scatter(g, level):
        for t in range(3):
            for steps in (1, 2, 3):
                pass_on(g, level, t, steps).start()

    def collected(g, level, t):
        out, inside, sem, rows = stages[level]
        for steps in (1, 2, 3):
            pass_on(g, level, t, steps).wait()
        own = pl.ds(pl.multiple_of(place[ORDERS[t][level]] * rows, rows), rows)
        total = out[g, t, own, :].astype(F32)
        for steps in (1, 2, 3):
            total = total + inside[g, t, steps - 1].astype(F32)
        return total

    def reduce_core(g):
        swap(g).wait()
        for t in range(3):
            a_out[g, t] = (term_ref[g, core, t].astype(F32) + core_in[g, t].astype(F32)).astype(BF16)
        scatter(g, 0)

    def reduce_a(g):
        for t in range(3):
            b_out[g, t] = collected(g, 0, t).astype(BF16)
        scatter(g, 1)

    def reduce_b(g):
        for t in range(3):
            c_out[g, t] = collected(g, 1, t)
        scatter(g, 2)

    def reduce_c(g):
        for t in range(3):
            wg_ref[:, pl.ds(pl.multiple_of(t * D + g * W, W), W)] = collected(g, 2, t) * 0.25

    @pl.loop(0, GROUPS)
    def _(g):
        @pl.when(g < GROUPS - 1)
        def _():
            project(g + 1)

        @pl.when(g > 1)
        def _():
            reduce_a(g - 2)

        adjoint(g).wait()
        for side in range(2):
            halo(g, side).wait()
        turn = g % 2
        for i, ref in enumerate((k_ref, v_ref)):
            ref[turn, 0] = kv_in[g, 0, i]
            ref[turn, 9] = kv_in[g, 1, i]

        @pl.loop(0, PAIRS)
        def _(pair):
            @pl.when((pair == 1) & (g > 1))
            def _():
                reduce_b(g - 2)

            @pl.when((pair == 1) & (g > 0))
            def _():
                merge(g - 1)
                terms(g - 1)

            attend_pair(g, pair)

        for side in range(2):
            back(g, side).start()

        @pl.when(g > 1)
        def _():
            reduce_c(g - 2)

        @pl.when(g > 0)
        def _():
            reduce_core(g - 1)

    last = GROUPS - 1
    total = None
    for g in range(GROUPS):
        part = nt(dq_ref[g], w_ref[0, :, g * W:(g + 1) * W])
        total = part if total is None else total + part
    mg_ref[...] = total.astype(BF16)
    pltpu.make_async_copy(mg_ref, mg_hbm, out_sem.at[0]).start()
    reduce_a(last - 1)
    merge(last)
    terms(last)

    def grid_grads(n):
        total = None
        for g in range(GROUPS):
            for i, ref in enumerate((dk_ref, dv_ref)):
                part = nt(ref[g], w_ref[1 + i, n * 256:(n + 1) * 256, g * W:(g + 1) * W])
                total = part if total is None else total + part
        gg_ref[:, n * 256:(n + 1) * 256] = total.astype(BF16)
        grid_out(n).start()

    def grid_out(n):
        return pltpu.make_async_copy(
            gg_ref.at[:, n * 256:(n + 1) * 256], gg_hbm.at[:, n * 256:(n + 1) * 256], out_sem.at[1 + n]
        )

    grid_grads(0)
    reduce_core(last)
    reduce_b(last - 1)
    grid_grads(1)
    reduce_c(last - 1)
    grid_grads(2)
    reduce_a(last)
    grid_grads(3)
    reduce_b(last)
    reduce_c(last)
    copy = pltpu.make_async_copy(wg_ref, wg_hbm, out_sem.at[5])
    copy.start()
    copy.wait()
    pltpu.make_async_copy(mg_ref, mg_hbm, out_sem.at[0]).wait()
    for n in range(4):
        grid_out(n).wait()


def on_device(grid_feat, mesh_feat, mesh_adjoint, w_query, w_key, w_value, block_grid, block_mask):
    anywhere = pl.BlockSpec(memory_space=pl.ANY)
    dma = pltpu.SemaphoreType.DMA
    grid_grad, mesh_grad, w_grad = pl.pallas_call(
        kernel,
        in_specs=[pl.BlockSpec(memory_space=pltpu.SMEM)] + [anywhere] * 7,
        out_specs=[anywhere] * 3,
        out_shape=[
            jax.ShapeDtypeStruct((1024, D), BF16),
            jax.ShapeDtypeStruct((512, D), BF16),
            jax.ShapeDtypeStruct((8, 3 * D), F32),
        ],
        scratch_shapes=[
            pltpu.VMEM((1024, D), BF16),
            pltpu.VMEM((512, D), BF16),
            pltpu.VMEM((D, 1024), BF16),
            pltpu.VMEM((D, 512), BF16),
            pltpu.VMEM((3, D, D), BF16),
            pltpu.VMEM((16, 128, 128), jnp.int32),
            pltpu.VMEM((4, 512, 128), F32),
            pltpu.VMEM((GROUPS, 512, W), BF16),
            pltpu.VMEM((2, 512, W), BF16),
            pltpu.VMEM((2, 10, 128, W), BF16),
            pltpu.VMEM((2, 10, 128, W), BF16),
            pltpu.VMEM((GROUPS, 512, W), BF16),
            pltpu.VMEM((GROUPS, 1024, W), BF16),
            pltpu.VMEM((GROUPS, 1024, W), BF16),
            pltpu.VMEM((17, 128, 128), F32),
            pltpu.VMEM((17, 128, 128), F32),
            pltpu.VMEM((2, 2, 2, 128, W), F32),
            pltpu.VMEM((GROUPS, 2, 2, 128, W), BF16),
            pltpu.VMEM((GROUPS, 2, 2, 128, W), BF16),
            pltpu.VMEM((GROUPS, 2, 2, 128, W), BF16),
            pltpu.VMEM((GROUPS, 2, 2, 128, W), BF16),
            pltpu.VMEM((GROUPS, 2, 3, 512, W), BF16),
            pltpu.VMEM((GROUPS, 3, 512, W), BF16),
            pltpu.VMEM((GROUPS, 3, 512, W), BF16),
            pltpu.VMEM((GROUPS, 3, 3, 128, W), BF16),
            pltpu.VMEM((GROUPS, 3, 128, W), BF16),
            pltpu.VMEM((GROUPS, 3, 3, 32, W), BF16),
            pltpu.VMEM((GROUPS, 3, 32, W), F32),
            pltpu.VMEM((GROUPS, 3, 3, 8, W), F32),
            pltpu.VMEM((8, 3 * D), F32),
            pltpu.VMEM((1024, D), BF16),
            pltpu.VMEM((512, D), BF16),
            pltpu.SMEM((16,), jnp.int32),
            pltpu.SMEM((40,), jnp.int32),
            dma((3,)),
            dma((GROUPS, 3)),
            dma((6,)),
            dma((2, GROUPS)),
            dma((2, GROUPS, 2)),
            dma((2, GROUPS, 2)),
            dma((2, GROUPS)),
            dma((2, GROUPS, 3, 3)),
            dma((2, GROUPS, 3, 3)),
            dma((2, GROUPS, 3, 3)),
        ],
        compiler_params=pltpu.CompilerParams(
            collective_id=0, has_side_effects=True, vmem_limit_bytes=62 << 20
        ),
        cost_estimate=pl.CostEstimate(flops=20 * 2**30, bytes_accessed=20 << 20, transcendentals=4 << 20),
    )(block_grid, grid_feat[0], mesh_feat[0], mesh_adjoint[0], w_query, w_key, w_value, block_mask)
    return (grid_grad[None], mesh_grad[None], w_grad)


def solution(mesh):
    placed = (
        P("sec", "space", None),
        P("sec", "space", None),
        P("sec", "space", None),
        P(),
        P(),
        P(),
        P("space"),
        P("space", None, None),
    )
    return jax.shard_map(
        on_device,
        mesh=mesh,
        in_specs=placed,
        out_specs=(P("sec", "space", None), P("sec", "space", None), P(("sec", "space"), None)),
        check_vma=False,
    )
```

```python
import jax
import jax.numpy as jnp
from jax import lax
from jax.experimental import pallas as pl
from jax.experimental.pallas import tpu as pltpu
from jax.sharding import PartitionSpec as P

F32, BF16 = jnp.float32, jnp.bfloat16
MESH = pl.DeviceIdType.MESH
D = 1024
GROUPS = 4
W = D // GROUPS
PAIRS = W // 128
BANDS = 32
ORDERS = ((0, 1, 2), (1, 0, 2), (2, 0, 1))


def nt(a, b):
    return lax.dot_general(a, b, (((1,), (1,)), ((), ())), preferred_element_type=F32)


def tn(a, b):
    return lax.dot_general(a, b, (((0,), (0,)), ((), ())), preferred_element_type=F32)


def nn(a, b):
    return lax.dot_general(a, b, (((1,), (0,)), ((), ())), preferred_element_type=F32)


def paired(x):
    left = lax.broadcasted_iota(jnp.int32, x.shape, 1) < 64
    zero = jnp.zeros_like(x)
    return jnp.concatenate([jnp.where(left, x, zero), jnp.where(left, zero, x)], axis=0)


def kernel(
    ids_ref, x_hbm, h_hbm, a_hbm, wq_hbm, wk_hbm, wv_hbm, mask_hbm,
    gg_hbm, mg_hbm, wg_hbm,
    x_ref, h_ref, xt_ref, ht_ref, w_ref, mask_ref, bias_ref, adj_ref, q_ref, k_ref, v_ref,
    dq_ref, dk_ref, dv_ref, dk_part, dv_part, edge_ref,
    kv_out, kv_in, dkv_out, dkv_in,
    term_ref, core_in, a_out, a_in, b_out, b_in, c_out, c_in, wg_ref, gg_ref, mg_ref,
    local_ref, lists_ref, load_sem, w_sem, out_sem, adj_sem, kv_sem, dkv_sem, core_sem, a_sem, b_sem, c_sem,
):
    sec = lax.axis_index("sec")
    band = lax.axis_index("space")
    core = band % 2
    gx = band // 8
    gy = (band // 2) % 4
    place = (sec, gx, gy)

    def space_of(x, y, c):
        return (x * 4 + y) * 2 + c

    def peer(axis, steps):
        z, x, y = place
        if axis == 0:
            return ((z + steps) % 4, band)
        if axis == 1:
            return (z, space_of((x + steps) % 4, y, core))
        return (z, space_of(x, (y + steps) % 4, core))

    sibling = (sec, space_of(gx, gy, 1 - core))
    up = (sec, (band + 1) % BANDS)
    down = (sec, (band + BANDS - 1) % BANDS)
    across = (sec, (band + BANDS + 2 * core - 1) % BANDS)

    def cols_of(g):
        return pl.ds(pl.multiple_of(g * W, W), W)

    def load(src, dst, i):
        return pltpu.make_async_copy(src, dst, load_sem.at[i])

    def load_w(g, i):
        return pltpu.make_async_copy(
            (wq_hbm, wk_hbm, wv_hbm)[i].at[:, cols_of(g)], w_ref.at[i, g], w_sem.at[g, i]
        )

    def remote(src, dst, sem, at, to):
        return pltpu.make_async_remote_copy(
            src_ref=src, dst_ref=dst, send_sem=sem.at[(0, *at)], recv_sem=sem.at[(1, *at)],
            device_id=to, device_id_type=MESH,
        )

    barrier = pltpu.get_barrier_semaphore()
    peers = [sibling, across] + [peer(axis, steps) for axis in range(3) for steps in (1, 2, 3)]
    for to in peers:
        pl.semaphore_signal(barrier, inc=1, device_id=to, device_id_type=MESH)
    load(x_hbm, x_ref, 0).start()
    for i in (1, 2):
        load_w(0, i).start()
    load(h_hbm, h_ref, 1).start()
    load_w(0, 0).start()
    pl.semaphore_wait(barrier, len(peers))

    def adjoint(g):
        return remote(a_hbm.at[:, cols_of(g)], adj_ref.at[g], adj_sem, (g,), peer(0, 3))

    for g in range(GROUPS):
        adjoint(g).start()

    def halo(g, side):
        return remote(kv_out.at[g, side], kv_in.at[g, 1 - side], kv_sem, (g, side), (down, up)[side])

    def project(g):
        turn = g % 2
        for i in (1, 2):
            load_w(g, i).wait()
            for r in range(4):
                own = nn(x_ref[r * 256:(r + 1) * 256], w_ref[i, g]).astype(BF16)
                (k_ref, v_ref)[i - 1][turn, 1 + 2 * r:3 + 2 * r] = own.reshape(2, 128, W)
                if r == 0:
                    kv_out[g, 0, i - 1] = own[:128]
                if r == 3:
                    kv_out[g, 1, i - 1] = own[128:]
        for side in range(2):
            halo(g, side).start()
        load_w(g, 0).wait()
        for r in range(2):
            rows = slice(r * 256, (r + 1) * 256)
            q_ref[turn, rows] = nn(h_ref[rows], w_ref[0, g]).astype(BF16) * 0.125

    load(x_hbm, x_ref, 0).wait()
    load(h_hbm, h_ref, 1).wait()
    load(mask_hbm, mask_ref, 2).start()
    for g in range(1, GROUPS):
        for i in range(3):
            load_w(g, i).start()
    project(0)

    @pl.loop(0, 8)
    def _(i):
        rows = pl.ds(pl.multiple_of(i * 128, 128), 128)
        xt_ref[:, rows] = x_ref[rows, :].T

    @pl.loop(0, 4)
    def _(i):
        rows = pl.ds(pl.multiple_of(i * 128, 128), 128)
        ht_ref[:, rows] = h_ref[rows, :].T

    load(mask_hbm, mask_ref, 2).wait()

    @pl.loop(0, 4)
    def _(m):
        for s in range(4):
            bias_ref[m, s * 128:(s + 1) * 128, :] = (mask_ref[m * 4 + s].astype(F32).T - 1.0) * 1e30

    dk_part[16] = jnp.zeros((128, 128), F32)
    dv_part[16] = jnp.zeros((128, 128), F32)

    for e in range(16):
        local_ref[e] = jnp.clip(ids_ref[e] - band * 8 + 1, 0, 9)
    for block in range(10):
        for m in range(4):
            at = 16
            for s in range(4):
                off = local_ref[m * 4 + s] - block
                at = at + (1 - jnp.minimum(off * off, 1)) * (m * 4 + s - 16)
            lists_ref[block * 4 + m] = jnp.clip(at, 0, 16)

    def attend(g, pair, m):
        turn = g % 2
        rows = slice(m * 128, (m + 1) * 128)
        cols = pl.ds(pl.multiple_of(pair * 128, 128), 128)
        blocks = [local_ref[m * 4 + s] for s in range(4)]
        keys = jnp.concatenate([k_ref[turn, b, :, cols] for b in blocks], axis=0)
        values = jnp.concatenate([v_ref[turn, b, :, cols] for b in blocks], axis=0)
        qq = paired(q_ref[turn, rows, cols])
        aa = paired(adj_ref[g, rows, cols])
        bias = bias_ref[m]
        bias = jnp.concatenate([bias, bias], axis=1)
        scores = nt(keys, qq) + bias
        top = jnp.max(scores, axis=0, keepdims=True)
        expo = jnp.exp(scores - top)
        probs = expo * (1.0 / jnp.sum(expo, axis=0, keepdims=True))
        probs_b = probs.astype(BF16)
        dprobs = nt(values, aa)
        delta = jnp.sum(probs_b.astype(F32) * dprobs, axis=0, keepdims=True)
        ds = (probs * (dprobs - delta)).astype(BF16)
        dv = nn(probs_b, aa)
        dk = nn(ds, qq)
        for s in range(4):
            dv_part[m * 4 + s] = dv[s * 128:(s + 1) * 128]
            dk_part[m * 4 + s] = dk[s * 128:(s + 1) * 128]
        dq = tn(keys, ds)
        dq = jnp.concatenate([dq[:64, :128], dq[64:, 128:]], axis=0) * 0.125
        dq_ref[g, rows, cols] = dq.T.astype(BF16)

    def gathered(part, block):
        found = [part[lists_ref[block * 4 + m]] for m in range(4)]
        return (found[0] + found[1]) + (found[2] + found[3])

    def attend_pair(g, pair):
        cols = pl.ds(pl.multiple_of(pair * 128, 128), 128)
        for m in range(4):
            attend(g, pair, m)
        for i, part in enumerate((dk_part, dv_part)):
            dkv_out[g, 0, i, :, cols] = gathered(part, 0).astype(BF16)
            dkv_out[g, 1, i, :, cols] = gathered(part, 9).astype(BF16)
            edge_ref[g % 2, 0, i, :, cols] = gathered(part, 1)
            edge_ref[g % 2, 1, i, :, cols] = gathered(part, 8)

        @pl.loop(1, 7)
        def _(block):
            rows = pl.ds(pl.multiple_of(block * 128, 128), 128)
            dk_ref[g, rows, cols] = gathered(dk_part, block + 1).astype(BF16)
            dv_ref[g, rows, cols] = gathered(dv_part, block + 1).astype(BF16)

    def back(g, side):
        return remote(dkv_out.at[g, side], dkv_in.at[g, 1 - side], dkv_sem, (g, side), (down, up)[side])

    def merge(g):
        for side in range(2):
            back(g, side).wait()
        for i, ref in enumerate((dk_ref, dv_ref)):
            ref[g, 0:128, :] = (edge_ref[g % 2, 0, i] + dkv_in[g, 0, i].astype(F32)).astype(BF16)
            ref[g, 896:1024, :] = (edge_ref[g % 2, 1, i] + dkv_in[g, 1, i].astype(F32)).astype(BF16)

    def swap(g):
        return remote(term_ref.at[g, 1 - core], core_in.at[g], core_sem, (g,), sibling)

    def terms(g, which=(0, 1, 2)):
        for t in which:
            strides = [(0, 64, 16)[axis] for axis in ORDERS[t]]
            for z in range(4):
                rows = slice(z * 256, (z + 1) * 256)
                if t == 0:
                    term = nn(ht_ref[rows], dq_ref[g])
                else:
                    term = nn(xt_ref[rows], (dk_ref, dv_ref)[t - 1][g])
                for c in range(2):
                    for n in range(0, 64, 2):
                        at = (n // 16, n // 4 % 4, n % 4)
                        if at[ORDERS[t].index(0)] != z:
                            continue
                        row = sum(a * b for a, b in zip(at, strides)) + c * 8
                        pieces = [term[row:row + 8], term[row + strides[2]:row + strides[2] + 8]]
                        term_ref[g, c, t, n * 8:n * 8 + 16, :] = jnp.concatenate(pieces, axis=0).astype(BF16)

    stages = ((a_out, a_in, a_sem, 128), (b_out, b_in, b_sem, 32), (c_out, c_in, c_sem, 8))

    def pass_on(g, level, t, steps):
        out, inside, sem, rows = stages[level]
        axis = ORDERS[t][level]
        first = pl.multiple_of((place[axis] + steps) % 4 * rows, rows)
        return remote(
            out.at[g, t, pl.ds(first, rows), :], inside.at[g, t, steps - 1], sem, (g,), peer(axis, steps)
        )

    def scatter(g, level):
        for steps in (2, 1, 3):
            for t in range(3):
                pass_on(g, level, t, steps).start()

    def arrived(g, level):
        _, inside, sem, _ = stages[level]
        for i in range(2):
            pltpu.make_async_copy(inside.at[g], inside.at[g], sem.at[i, g]).wait()

    def collected(g, level, t):
        out, inside, sem, rows = stages[level]
        own = pl.ds(pl.multiple_of(place[ORDERS[t][level]] * rows, rows), rows)
        total = out[g, t, own, :].astype(F32)
        for steps in (1, 2, 3):
            total = total + inside[g, t, steps - 1].astype(F32)
        return total

    def reduce_core(g):
        swap(g).wait()
        for t in range(3):
            a_out[g, t] = (term_ref[g, core, t].astype(F32) + core_in[g, t].astype(F32)).astype(BF16)
        scatter(g, 0)

    def reduce_a(g):
        arrived(g, 0)
        for t in range(3):
            b_out[g, t] = collected(g, 0, t).astype(BF16)
        scatter(g, 1)

    def reduce_b(g):
        arrived(g, 1)
        for t in range(3):
            c_out[g, t] = collected(g, 1, t)
        scatter(g, 2)

    def reduce_c(g):
        arrived(g, 2)
        for t in range(3):
            wg_ref[:, pl.ds(pl.multiple_of(t * D + g * W, W), W)] = collected(g, 2, t) * 0.25

    @pl.loop(0, GROUPS)
    def _(g):
        @pl.when(g < GROUPS - 1)
        def _():
            project(g + 1)

        adjoint(g).wait()
        for side in range(2):
            halo(g, side).wait()
        turn = g % 2
        for i, ref in enumerate((k_ref, v_ref)):
            ref[turn, 0] = kv_in[g, 0, i]
            ref[turn, 9] = kv_in[g, 1, i]

        @pl.loop(0, PAIRS)
        def _(pair):
            @pl.when((pair == 1) & (g > 2))
            def _():
                reduce_c(g - 3)

            @pl.when((pair == 1) & (g > 1))
            def _():
                reduce_a(g - 2)

            @pl.when((pair == 1) & (g > 0))
            def _():
                merge(g - 1)
                terms(g - 1)
                swap(g - 1).start()

            attend_pair(g, pair)

        for side in range(2):
            back(g, side).start()

        @pl.when(g > 1)
        def _():
            reduce_b(g - 2)

        @pl.when(g > 0)
        def _():
            reduce_core(g - 1)

    last = GROUPS - 1
    terms(last, (0,))
    for r in range(2):
        rows = slice(r * 256, (r + 1) * 256)
        for n in range(4):
            cols = slice(n * 256, (n + 1) * 256)
            total = None
            for g in range(GROUPS):
                part = nt(dq_ref[g, rows], w_ref[0, g, cols])
                total = part if total is None else total + part
            mg_ref[rows, cols] = total.astype(BF16)
    pltpu.make_async_copy(mg_ref, mg_hbm, out_sem.at[0]).start()
    merge(last)
    terms(last, (1, 2))
    swap(last).start()

    def grid_grads(n):
        cols = slice(n * 256, (n + 1) * 256)
        for r in range(4):
            rows = slice(r * 256, (r + 1) * 256)
            total = None
            for g in range(GROUPS):
                for i, ref in enumerate((dk_ref, dv_ref)):
                    part = nt(ref[g, rows], w_ref[1 + i, g, cols])
                    total = part if total is None else total + part
            gg_ref[rows, cols] = total.astype(BF16)
        grid_out(n).start()

    def grid_out(n):
        return pltpu.make_async_copy(
            gg_ref.at[:, n * 256:(n + 1) * 256], gg_hbm.at[:, n * 256:(n + 1) * 256], out_sem.at[1 + n]
        )

    grid_grads(0)
    reduce_a(last - 1)
    grid_grads(1)
    reduce_core(last)
    reduce_c(last - 2)
    reduce_b(last - 1)
    grid_grads(2)
    grid_grads(3)
    reduce_a(last)
    reduce_c(last - 1)
    reduce_b(last)
    reduce_c(last)
    copy = pltpu.make_async_copy(wg_ref, wg_hbm, out_sem.at[5])
    copy.start()
    copy.wait()
    pltpu.make_async_copy(mg_ref, mg_hbm, out_sem.at[0]).wait()
    for n in range(4):
        grid_out(n).wait()


def hand_out(gg, mg, wg, gg_out, mg_out, wg_out, gg_ref, mg_ref, wg_ref, sem):
    steps = []
    for src, held, dst, parts in ((gg, gg_ref, gg_out, 4), (mg, mg_ref, mg_out, 2), (wg, wg_ref, wg_out, 1)):
        rows = src.shape[0] // parts
        for part in range(parts):
            at = pl.ds(part * rows, rows)
            n = len(steps)
            steps.append((
                pltpu.make_async_copy(src.at[at], held.at[at], sem.at[0, n]),
                pltpu.make_async_copy(held.at[at], dst.at[at], sem.at[1, n]),
            ))
    for come, _ in steps:
        come.start()
    for come, go in steps:
        come.wait()
        go.start()
    for _, go in steps:
        go.wait()


def on_device(grid_feat, mesh_feat, mesh_adjoint, w_query, w_key, w_value, block_grid, block_mask):
    anywhere = pl.BlockSpec(memory_space=pl.ANY)
    dma = pltpu.SemaphoreType.DMA
    grid_grad, mesh_grad, w_grad = pl.pallas_call(
        kernel,
        in_specs=[pl.BlockSpec(memory_space=pltpu.SMEM)] + [anywhere] * 7,
        out_specs=[anywhere] * 3,
        out_shape=[
            jax.ShapeDtypeStruct((1024, D), BF16),
            jax.ShapeDtypeStruct((512, D), BF16),
            jax.ShapeDtypeStruct((8, 3 * D), F32),
        ],
        scratch_shapes=[
            pltpu.VMEM((1024, D), BF16),
            pltpu.VMEM((512, D), BF16),
            pltpu.VMEM((D, 1024), BF16),
            pltpu.VMEM((D, 512), BF16),
            pltpu.VMEM((3, GROUPS, D, W), BF16),
            pltpu.VMEM((16, 128, 128), jnp.int32),
            pltpu.VMEM((4, 512, 128), F32),
            pltpu.VMEM((GROUPS, 512, W), BF16),
            pltpu.VMEM((2, 512, W), BF16),
            pltpu.VMEM((2, 10, 128, W), BF16),
            pltpu.VMEM((2, 10, 128, W), BF16),
            pltpu.VMEM((GROUPS, 512, W), BF16),
            pltpu.VMEM((GROUPS, 1024, W), BF16),
            pltpu.VMEM((GROUPS, 1024, W), BF16),
            pltpu.VMEM((17, 128, 128), F32),
            pltpu.VMEM((17, 128, 128), F32),
            pltpu.VMEM((2, 2, 2, 128, W), F32),
            pltpu.VMEM((GROUPS, 2, 2, 128, W), BF16),
            pltpu.VMEM((GROUPS, 2, 2, 128, W), BF16),
            pltpu.VMEM((GROUPS, 2, 2, 128, W), BF16),
            pltpu.VMEM((GROUPS, 2, 2, 128, W), BF16),
            pltpu.VMEM((GROUPS, 2, 3, 512, W), BF16),
            pltpu.VMEM((GROUPS, 3, 512, W), BF16),
            pltpu.VMEM((GROUPS, 3, 512, W), BF16),
            pltpu.VMEM((GROUPS, 3, 3, 128, W), BF16),
            pltpu.VMEM((GROUPS, 3, 128, W), BF16),
            pltpu.VMEM((GROUPS, 3, 3, 32, W), BF16),
            pltpu.VMEM((GROUPS, 3, 32, W), F32),
            pltpu.VMEM((GROUPS, 3, 3, 8, W), F32),
            pltpu.VMEM((8, 3 * D), F32),
            pltpu.VMEM((1024, D), BF16),
            pltpu.VMEM((512, D), BF16),
            pltpu.SMEM((16,), jnp.int32),
            pltpu.SMEM((40,), jnp.int32),
            dma((3,)),
            dma((GROUPS, 3)),
            dma((6,)),
            dma((2, GROUPS)),
            dma((2, GROUPS, 2)),
            dma((2, GROUPS, 2)),
            dma((2, GROUPS)),
            dma((2, GROUPS)),
            dma((2, GROUPS)),
            dma((2, GROUPS)),
        ],
        compiler_params=pltpu.CompilerParams(
            collective_id=0, has_side_effects=True, vmem_limit_bytes=62 << 20
        ),
        cost_estimate=pl.CostEstimate(flops=20 * 2**30, bytes_accessed=20 << 20, transcendentals=4 << 20),
    )(block_grid, grid_feat[0], mesh_feat[0], mesh_adjoint[0], w_query, w_key, w_value, block_mask)
    results = (grid_grad, mesh_grad, w_grad)
    grid_grad, mesh_grad, w_grad = pl.pallas_call(
        hand_out,
        in_specs=[anywhere] * 3,
        out_specs=[anywhere] * 3,
        out_shape=[jax.ShapeDtypeStruct(r.shape, r.dtype) for r in results],
        scratch_shapes=[pltpu.VMEM(r.shape, r.dtype) for r in results] + [dma((2, 7))],
    )(*results)
    return (grid_grad[None], mesh_grad[None], w_grad)


def solution(mesh):
    placed = (
        P("sec", "space", None),
        P("sec", "space", None),
        P("sec", "space", None),
        P(),
        P(),
        P(),
        P("space"),
        P("space", None, None),
    )
    return jax.shard_map(
        on_device,
        mesh=mesh,
        in_specs=placed,
        out_specs=(P("sec", "space", None), P("sec", "space", None), P(("sec", "space"), None)),
        check_vma=False,
    )
```

```python
import jax
import jax.numpy as jnp
from jax import lax
from jax.experimental import pallas as pl
from jax.experimental.pallas import tpu as pltpu
from jax.sharding import PartitionSpec as P

F32, BF16 = jnp.float32, jnp.bfloat16
MESH = pl.DeviceIdType.MESH
D = 1024
GROUPS = 4
W = D // GROUPS
PAIRS = W // 128
BANDS = 32
ORDERS = ((0, 1, 2), (1, 0, 2), (2, 0, 1))


def nt(a, b):
    return lax.dot_general(a, b, (((1,), (1,)), ((), ())), preferred_element_type=F32)


def tn(a, b):
    return lax.dot_general(a, b, (((0,), (0,)), ((), ())), preferred_element_type=F32)


def nn(a, b):
    return lax.dot_general(a, b, (((1,), (0,)), ((), ())), preferred_element_type=F32)


def paired(x):
    left = lax.broadcasted_iota(jnp.int32, x.shape, 1) < 64
    zero = jnp.zeros_like(x)
    return jnp.concatenate([jnp.where(left, x, zero), jnp.where(left, zero, x)], axis=0)


def kernel(
    ids_ref, x_hbm, h_hbm, a_hbm, wq_hbm, wk_hbm, wv_hbm, mask_hbm,
    gg_hbm, mg_hbm, wg_hbm,
    x_ref, h_ref, xt_ref, ht_ref, w_ref, mask_ref, bias_ref, adj_ref, q_ref, k_ref, v_ref,
    dq_ref, dk_ref, dv_ref, dk_part, dv_part, edge_ref,
    kv_out, kv_in, dkv_out, dkv_in,
    term_ref, core_in, a_out, a_in, b_out, b_in, c_out, c_in, wg_ref, gg_ref, mg_ref,
    local_ref, lists_ref, load_sem, w_sem, out_sem, adj_sem, kv_sem, dkv_sem, core_sem, a_sem, b_sem, c_sem,
):
    sec = lax.axis_index("sec")
    band = lax.axis_index("space")
    core = band % 2
    gx = band // 8
    gy = (band // 2) % 4
    place = (sec, gx, gy)

    def space_of(x, y, c):
        return (x * 4 + y) * 2 + c

    def peer(axis, steps):
        z, x, y = place
        if axis == 0:
            return ((z + steps) % 4, band)
        if axis == 1:
            return (z, space_of((x + steps) % 4, y, core))
        return (z, space_of(x, (y + steps) % 4, core))

    near = {(axis, steps): peer(axis, steps) for axis in range(3) for steps in (1, 2, 3)}
    ahead = {(axis, steps): (place[axis] + steps) % 4 for axis in range(3) for steps in (1, 2, 3)}
    sibling = (sec, space_of(gx, gy, 1 - core))
    up = (sec, (band + 1) % BANDS)
    down = (sec, (band + BANDS - 1) % BANDS)
    across = (sec, (band + BANDS + 2 * core - 1) % BANDS)

    def cols_of(g):
        return pl.ds(pl.multiple_of(g * W, W), W)

    def load(src, dst, i):
        return pltpu.make_async_copy(src, dst, load_sem.at[i])

    def load_w(g, i):
        return pltpu.make_async_copy(
            (wq_hbm, wk_hbm, wv_hbm)[i].at[:, cols_of(g)], w_ref.at[i, g], w_sem.at[g, i]
        )

    def remote(src, dst, sem, at, to):
        return pltpu.make_async_remote_copy(
            src_ref=src, dst_ref=dst, send_sem=sem.at[(0, *at)], recv_sem=sem.at[(1, *at)],
            device_id=to, device_id_type=MESH,
        )

    barrier = pltpu.get_barrier_semaphore()
    peers = [sibling, across] + [*near.values()]
    for to in peers:
        pl.semaphore_signal(barrier, inc=1, device_id=to, device_id_type=MESH)
    load(x_hbm, x_ref, 0).start()
    for i in (1, 2):
        load_w(0, i).start()
    load(h_hbm, h_ref, 1).start()
    load_w(0, 0).start()
    pl.semaphore_wait(barrier, len(peers))

    def adjoint(g):
        return remote(a_hbm.at[:, cols_of(g)], adj_ref.at[g], adj_sem, (g,), near[0, 3])

    adjoint(0).start()

    def halo(g, side):
        return remote(kv_out.at[g, side], kv_in.at[g, 1 - side], kv_sem, (g, side), (down, up)[side])

    def project(g):
        turn = g % 2
        for i in (1, 2):
            load_w(g, i).wait()
            for r in range(4):
                own = nn(x_ref[r * 256:(r + 1) * 256], w_ref[i, g]).astype(BF16)
                (k_ref, v_ref)[i - 1][turn, 1 + 2 * r:3 + 2 * r] = own.reshape(2, 128, W)
                if r == 0:
                    kv_out[g, 0, i - 1] = own[:128]
                if r == 3:
                    kv_out[g, 1, i - 1] = own[128:]
        for side in range(2):
            halo(g, side).start()
        load_w(g, 0).wait()
        for r in range(2):
            rows = slice(r * 256, (r + 1) * 256)
            q_ref[turn, rows] = nn(h_ref[rows], w_ref[0, g]).astype(BF16) * 0.125

    load(x_hbm, x_ref, 0).wait()
    load(h_hbm, h_ref, 1).wait()
    load(mask_hbm, mask_ref, 2).start()
    for g in range(1, GROUPS):
        for i in range(3):
            load_w(g, i).start()
    project(0)

    @pl.loop(0, 8)
    def _(i):
        rows = pl.ds(pl.multiple_of(i * 128, 128), 128)
        xt_ref[:, rows] = x_ref[rows, :].T

    @pl.loop(0, 4)
    def _(i):
        rows = pl.ds(pl.multiple_of(i * 128, 128), 128)
        ht_ref[:, rows] = h_ref[rows, :].T

    load(mask_hbm, mask_ref, 2).wait()

    @pl.loop(0, 4)
    def _(m):
        for s in range(4):
            bias_ref[m, s * 128:(s + 1) * 128, :] = (mask_ref[m * 4 + s].astype(F32).T - 1.0) * 1e30

    dk_part[16] = jnp.zeros((128, 128), F32)
    dv_part[16] = jnp.zeros((128, 128), F32)

    for e in range(16):
        local_ref[e] = jnp.clip(ids_ref[e] - band * 8 + 1, 0, 9)
    for block in range(10):
        for m in range(4):
            at = 16
            for s in range(4):
                off = local_ref[m * 4 + s] - block
                at = at + (1 - jnp.minimum(off * off, 1)) * (m * 4 + s - 16)
            lists_ref[block * 4 + m] = jnp.clip(at, 0, 16)

    def operands(g, pair, m):
        turn = g % 2
        rows = slice(m * 128, (m + 1) * 128)
        cols = pl.ds(pl.multiple_of(pair * 128, 128), 128)
        blocks = [local_ref[m * 4 + s] for s in range(4)]
        keys = jnp.concatenate([k_ref[turn, b, :, cols] for b in blocks], axis=0)
        values = jnp.concatenate([v_ref[turn, b, :, cols] for b in blocks], axis=0)
        qq = paired(q_ref[turn, rows, cols])
        aa = paired(adj_ref[g, rows, cols])
        return keys, qq, aa, nt(keys, qq), nt(values, aa)

    def weigh(m, scores, dprobs):
        bias = bias_ref[m]
        bias = jnp.concatenate([bias, bias], axis=1)
        scores = scores + bias
        top = jnp.max(scores, axis=0, keepdims=True)
        expo = jnp.exp(scores - top)
        probs = expo * (1.0 / jnp.sum(expo, axis=0, keepdims=True))
        probs_b = probs.astype(BF16)
        delta = jnp.sum(probs_b.astype(F32) * dprobs, axis=0, keepdims=True)
        return probs_b, (probs * (dprobs - delta)).astype(BF16)

    def spread(g, pair, m, keys, qq, aa, probs_b, ds):
        rows = slice(m * 128, (m + 1) * 128)
        cols = pl.ds(pl.multiple_of(pair * 128, 128), 128)
        dv = nn(probs_b, aa)
        dk = nn(ds, qq)
        for s in range(4):
            dv_part[m * 4 + s] = dv[s * 128:(s + 1) * 128]
            dk_part[m * 4 + s] = dk[s * 128:(s + 1) * 128]
        dq = tn(keys, ds)
        dq = jnp.concatenate([dq[:64, :128], dq[64:, 128:]], axis=0) * 0.125
        dq_ref[g, rows, cols] = dq.T.astype(BF16)

    def gathered(part, block):
        found = [part[lists_ref[block * 4 + m]] for m in range(4)]
        return (found[0] + found[1]) + (found[2] + found[3])

    def attend_pair(g, pair):
        cols = pl.ds(pl.multiple_of(pair * 128, 128), 128)
        ready = operands(g, pair, 0)
        done = None
        for m in range(4):
            keys, qq, aa, scores, dprobs = ready
            if m < 3:
                ready = operands(g, pair, m + 1)
            weighed = weigh(m, scores, dprobs)
            if done is not None:
                spread(g, pair, m - 1, *done)
            done = (keys, qq, aa, *weighed)
        spread(g, pair, 3, *done)
        for i, part in enumerate((dk_part, dv_part)):
            dkv_out[g, 0, i, :, cols] = gathered(part, 0).astype(BF16)
            dkv_out[g, 1, i, :, cols] = gathered(part, 9).astype(BF16)
            edge_ref[g % 2, 0, i, :, cols] = gathered(part, 1)
            edge_ref[g % 2, 1, i, :, cols] = gathered(part, 8)

        @pl.loop(1, 7)
        def _(block):
            rows = pl.ds(pl.multiple_of(block * 128, 128), 128)
            dk_ref[g, rows, cols] = gathered(dk_part, block + 1).astype(BF16)
            dv_ref[g, rows, cols] = gathered(dv_part, block + 1).astype(BF16)

    def back(g, side):
        return remote(dkv_out.at[g, side], dkv_in.at[g, 1 - side], dkv_sem, (g, side), (down, up)[side])

    def merge(g):
        for side in range(2):
            back(g, side).wait()
        for i, ref in enumerate((dk_ref, dv_ref)):
            ref[g, 0:128, :] = (edge_ref[g % 2, 0, i] + dkv_in[g, 0, i].astype(F32)).astype(BF16)
            ref[g, 896:1024, :] = (edge_ref[g % 2, 1, i] + dkv_in[g, 1, i].astype(F32)).astype(BF16)

    def swap(g):
        return remote(term_ref.at[g, 1 - core], core_in.at[g], core_sem, (g,), sibling)

    def terms(g, which=(0, 1, 2)):
        for t in which:
            strides = [(0, 64, 16)[axis] for axis in ORDERS[t]]
            for z in range(4):
                rows = slice(z * 256, (z + 1) * 256)
                if t == 0:
                    term = nn(ht_ref[rows], dq_ref[g])
                else:
                    term = nn(xt_ref[rows], (dk_ref, dv_ref)[t - 1][g])
                for c in range(2):
                    for n in range(0, 64, 2):
                        at = (n // 16, n // 4 % 4, n % 4)
                        if at[ORDERS[t].index(0)] != z:
                            continue
                        row = sum(a * b for a, b in zip(at, strides)) + c * 8
                        pieces = [term[row:row + 8], term[row + strides[2]:row + strides[2] + 8]]
                        term_ref[g, c, t, n * 8:n * 8 + 16, :] = jnp.concatenate(pieces, axis=0).astype(BF16)

    stages = ((a_out, a_in, a_sem, 128), (b_out, b_in, b_sem, 32), (c_out, c_in, c_sem, 8))

    bundles = (((0, 1), (1, 2), (2, 3)), ((0, 1), (1, 3)), ((0, 2), (2, 3)))

    def pass_on(g, level, bundle, steps):
        out, inside, sem, rows = stages[level]
        axis = ORDERS[bundle[0]][level]
        both = pl.ds(bundle[0], bundle[1] - bundle[0])
        first = pl.multiple_of(ahead[axis, steps] * rows, rows)
        return remote(
            out.at[g, both, pl.ds(first, rows), :], inside.at[g, steps - 1, both], sem, (g,), near[axis, steps]
        )

    def scatter(g, level, which=(0, 1, 2)):
        for steps in (2, 1, 3):
            for n, bundle in enumerate(bundles[level]):
                if n in which:
                    pass_on(g, level, bundle, steps).start()

    def arrived(g, level):
        _, inside, sem, _ = stages[level]
        for i in range(2):
            pltpu.make_async_copy(inside.at[g], inside.at[g], sem.at[i, g]).wait()

    def collected(g, level, t):
        out, inside, sem, rows = stages[level]
        own = pl.ds(pl.multiple_of(place[ORDERS[t][level]] * rows, rows), rows)
        total = out[g, t, own, :].astype(F32)
        for steps in (1, 2, 3):
            total = total + inside[g, steps - 1, t].astype(F32)
        return total

    def join_core(g, t):
        a_out[g, t] = (term_ref[g, core, t].astype(F32) + core_in[g, t].astype(F32)).astype(BF16)

    def reduce_core(g):
        swap(g).wait()
        for t in range(3):
            join_core(g, t)
        scatter(g, 0)

    def swap_one(t):
        return remote(
            term_ref.at[GROUPS - 1, 1 - core, t], core_in.at[GROUPS - 1, t], core_sem, (GROUPS - 1 + t,), sibling
        )

    def reduce_core_one(t):
        swap_one(t).wait()
        join_core(GROUPS - 1, t)
        scatter(GROUPS - 1, 0, (t,))

    def reduce_a(g):
        arrived(g, 0)
        for t in range(3):
            b_out[g, t] = collected(g, 0, t).astype(BF16)
        scatter(g, 1)

    def reduce_b(g):
        arrived(g, 1)
        for t in range(3):
            c_out[g, t] = collected(g, 1, t)
        scatter(g, 2)

    def reduce_c(g):
        arrived(g, 2)
        for t in range(3):
            wg_ref[:, pl.ds(pl.multiple_of(t * D + g * W, W), W)] = collected(g, 2, t) * 0.25

    @pl.loop(0, GROUPS)
    def _(g):
        @pl.when(g < GROUPS - 1)
        def _():
            project(g + 1)

        adjoint(g).wait()

        @pl.when(g < GROUPS - 1)
        def _():
            adjoint(g + 1).start()

        for side in range(2):
            halo(g, side).wait()
        turn = g % 2
        for i, ref in enumerate((k_ref, v_ref)):
            ref[turn, 0] = kv_in[g, 0, i]
            ref[turn, 9] = kv_in[g, 1, i]

        @pl.loop(0, PAIRS)
        def _(pair):
            @pl.when((pair == 1) & (g > 2))
            def _():
                reduce_c(g - 3)

            @pl.when((pair == 1) & (g > 1))
            def _():
                reduce_a(g - 2)

            @pl.when((pair == 1) & (g > 0))
            def _():
                merge(g - 1)
                terms(g - 1)
                swap(g - 1).start()

            attend_pair(g, pair)

        for side in range(2):
            back(g, side).start()

        @pl.when(g > 1)
        def _():
            reduce_b(g - 2)

        @pl.when(g > 0)
        def _():
            reduce_core(g - 1)

    last = GROUPS - 1
    terms(last, (0,))
    swap_one(0).start()
    for r in range(2):
        rows = slice(r * 256, (r + 1) * 256)
        for n in range(4):
            cols = slice(n * 256, (n + 1) * 256)
            total = None
            for g in range(GROUPS):
                part = nt(dq_ref[g, rows], w_ref[0, g, cols])
                total = part if total is None else total + part
            mg_ref[rows, cols] = total.astype(BF16)
    pltpu.make_async_copy(mg_ref, mg_hbm, out_sem.at[0]).start()
    merge(last)
    for t in (1, 2):
        terms(last, (t,))
        swap_one(t).start()

    def grid_grads(n):
        cols = slice(n * 256, (n + 1) * 256)
        for r in range(4):
            rows = slice(r * 256, (r + 1) * 256)
            total = None
            for g in range(GROUPS):
                for i, ref in enumerate((dk_ref, dv_ref)):
                    part = nt(ref[g, rows], w_ref[1 + i, g, cols])
                    total = part if total is None else total + part
            gg_ref[rows, cols] = total.astype(BF16)
        grid_out(n).start()

    def grid_out(n):
        return pltpu.make_async_copy(
            gg_ref.at[:, n * 256:(n + 1) * 256], gg_hbm.at[:, n * 256:(n + 1) * 256], out_sem.at[1 + n]
        )

    reduce_core_one(0)
    grid_grads(0)
    reduce_core_one(1)
    reduce_a(last - 1)
    reduce_core_one(2)
    grid_grads(1)
    reduce_c(last - 2)
    reduce_b(last - 1)
    grid_grads(2)
    grid_grads(3)
    reduce_a(last)
    reduce_c(last - 1)
    reduce_b(last)
    reduce_c(last)
    copy = pltpu.make_async_copy(wg_ref, wg_hbm, out_sem.at[5])
    copy.start()
    copy.wait()
    pltpu.make_async_copy(mg_ref, mg_hbm, out_sem.at[0]).wait()
    for n in range(4):
        grid_out(n).wait()


def hand_out(gg, mg, wg, gg_out, mg_out, wg_out, gg_ref, mg_ref, wg_ref, sem):
    steps = []
    for src, held, dst, parts in ((gg, gg_ref, gg_out, 4), (mg, mg_ref, mg_out, 2), (wg, wg_ref, wg_out, 1)):
        rows = src.shape[0] // parts
        for part in range(parts):
            at = pl.ds(part * rows, rows)
            n = len(steps)
            steps.append((
                pltpu.make_async_copy(src.at[at], held.at[at], sem.at[0, n]),
                pltpu.make_async_copy(held.at[at], dst.at[at], sem.at[1, n]),
            ))
    for come, _ in steps:
        come.start()
    for come, go in steps:
        come.wait()
        go.start()
    for _, go in steps:
        go.wait()


def on_device(grid_feat, mesh_feat, mesh_adjoint, w_query, w_key, w_value, block_grid, block_mask):
    anywhere = pl.BlockSpec(memory_space=pl.ANY)
    dma = pltpu.SemaphoreType.DMA
    grid_grad, mesh_grad, w_grad = pl.pallas_call(
        kernel,
        in_specs=[pl.BlockSpec(memory_space=pltpu.SMEM)] + [anywhere] * 7,
        out_specs=[anywhere] * 3,
        out_shape=[
            jax.ShapeDtypeStruct((1024, D), BF16),
            jax.ShapeDtypeStruct((512, D), BF16),
            jax.ShapeDtypeStruct((8, 3 * D), F32),
        ],
        scratch_shapes=[
            pltpu.VMEM((1024, D), BF16),
            pltpu.VMEM((512, D), BF16),
            pltpu.VMEM((D, 1024), BF16),
            pltpu.VMEM((D, 512), BF16),
            pltpu.VMEM((3, GROUPS, D, W), BF16),
            pltpu.VMEM((16, 128, 128), jnp.int32),
            pltpu.VMEM((4, 512, 128), F32),
            pltpu.VMEM((GROUPS, 512, W), BF16),
            pltpu.VMEM((2, 512, W), BF16),
            pltpu.VMEM((2, 10, 128, W), BF16),
            pltpu.VMEM((2, 10, 128, W), BF16),
            pltpu.VMEM((GROUPS, 512, W), BF16),
            pltpu.VMEM((GROUPS, 1024, W), BF16),
            pltpu.VMEM((GROUPS, 1024, W), BF16),
            pltpu.VMEM((17, 128, 128), F32),
            pltpu.VMEM((17, 128, 128), F32),
            pltpu.VMEM((2, 2, 2, 128, W), F32),
            pltpu.VMEM((GROUPS, 2, 2, 128, W), BF16),
            pltpu.VMEM((GROUPS, 2, 2, 128, W), BF16),
            pltpu.VMEM((GROUPS, 2, 2, 128, W), BF16),
            pltpu.VMEM((GROUPS, 2, 2, 128, W), BF16),
            pltpu.VMEM((GROUPS, 2, 3, 512, W), BF16),
            pltpu.VMEM((GROUPS, 3, 512, W), BF16),
            pltpu.VMEM((GROUPS, 3, 512, W), BF16),
            pltpu.VMEM((GROUPS, 3, 3, 128, W), BF16),
            pltpu.VMEM((GROUPS, 3, 128, W), BF16),
            pltpu.VMEM((GROUPS, 3, 3, 32, W), BF16),
            pltpu.VMEM((GROUPS, 3, 32, W), F32),
            pltpu.VMEM((GROUPS, 3, 3, 8, W), F32),
            pltpu.VMEM((8, 3 * D), F32),
            pltpu.VMEM((1024, D), BF16),
            pltpu.VMEM((512, D), BF16),
            pltpu.SMEM((16,), jnp.int32),
            pltpu.SMEM((40,), jnp.int32),
            dma((3,)),
            dma((GROUPS, 3)),
            dma((6,)),
            dma((2, GROUPS)),
            dma((2, GROUPS, 2)),
            dma((2, GROUPS, 2)),
            dma((2, GROUPS + 2)),
            dma((2, GROUPS)),
            dma((2, GROUPS)),
            dma((2, GROUPS)),
        ],
        compiler_params=pltpu.CompilerParams(
            collective_id=0, has_side_effects=True, vmem_limit_bytes=62 << 20
        ),
        cost_estimate=pl.CostEstimate(flops=20 * 2**30, bytes_accessed=20 << 20, transcendentals=4 << 20),
    )(block_grid, grid_feat[0], mesh_feat[0], mesh_adjoint[0], w_query, w_key, w_value, block_mask)
    results = (grid_grad, mesh_grad, w_grad)
    grid_grad, mesh_grad, w_grad = pl.pallas_call(
        hand_out,
        in_specs=[anywhere] * 3,
        out_specs=[anywhere] * 3,
        out_shape=[jax.ShapeDtypeStruct(r.shape, r.dtype) for r in results],
        scratch_shapes=[pltpu.VMEM(r.shape, r.dtype) for r in results] + [dma((2, 7))],
    )(*results)
    return (grid_grad[None], mesh_grad[None], w_grad)


def solution(mesh):
    placed = (
        P("sec", "space", None),
        P("sec", "space", None),
        P("sec", "space", None),
        P(),
        P(),
        P(),
        P("space"),
        P("space", None, None),
    )
    return jax.shard_map(
        on_device,
        mesh=mesh,
        in_specs=placed,
        out_specs=(P("sec", "space", None), P("sec", "space", None), P(("sec", "space"), None)),
        check_vma=False,
    )
```

```python
import jax
import jax.numpy as jnp
from jax import lax
from jax.experimental import pallas as pl
from jax.experimental.pallas import tpu as pltpu
from jax.sharding import PartitionSpec as P

F32, BF16 = jnp.float32, jnp.bfloat16
MESH = pl.DeviceIdType.MESH
D = 1024
GROUPS = 4
W = D // GROUPS
PAIRS = W // 128
BANDS = 32
ORDERS = ((0, 1, 2), (1, 0, 2), (2, 0, 1))


def nt(a, b):
    return lax.dot_general(a, b, (((1,), (1,)), ((), ())), preferred_element_type=F32)


def tn(a, b):
    return lax.dot_general(a, b, (((0,), (0,)), ((), ())), preferred_element_type=F32)


def nn(a, b):
    return lax.dot_general(a, b, (((1,), (0,)), ((), ())), preferred_element_type=F32)


def paired(x):
    left = lax.broadcasted_iota(jnp.int32, x.shape, 1) < 64
    zero = jnp.zeros_like(x)
    return jnp.concatenate([jnp.where(left, x, zero), jnp.where(left, zero, x)], axis=0)


def kernel(
    ids_ref, x_hbm, h_hbm, a_hbm, wq_hbm, wk_hbm, wv_hbm, mask_hbm,
    gg_hbm, mg_hbm, wg_hbm,
    x_ref, h_ref, xt_ref, ht_ref, w_ref, mask_ref, bias_ref, adj_ref, q_ref, k_ref, v_ref,
    dq_ref, dk_ref, dv_ref, dk_part, dv_part, edge_ref,
    kv_out, kv_in, dkv_out, dkv_in,
    term_ref, core_in, a_out, a_in, b_out, b_in, c_out, c_in, wg_ref, gg_ref, mg_ref,
    xh_ref, xht_ref, xh_sem, local_ref, lists_ref, load_sem, w_sem, out_sem, adj_sem, kv_sem, dkv_sem, core_sem, a_sem, b_sem, c_sem,
):
    sec = lax.axis_index("sec")
    band = lax.axis_index("space")
    core = band % 2
    gx = band // 8
    gy = (band // 2) % 4
    place = (sec, gx, gy)

    def space_of(x, y, c):
        return (x * 4 + y) * 2 + c

    def peer(axis, steps):
        z, x, y = place
        if axis == 0:
            return ((z + steps) % 4, band)
        if axis == 1:
            return (z, space_of((x + steps) % 4, y, core))
        return (z, space_of(x, (y + steps) % 4, core))

    near = {(axis, steps): peer(axis, steps) for axis in range(3) for steps in (1, 2, 3)}
    ahead = {(axis, steps): (place[axis] + steps) % 4 for axis in range(3) for steps in (1, 2, 3)}
    sibling = (sec, space_of(gx, gy, 1 - core))
    up = (sec, (band + 1) % BANDS)
    down = (sec, (band + BANDS - 1) % BANDS)
    across = (sec, (band + BANDS + 2 * core - 1) % BANDS)

    def cols_of(g):
        return pl.ds(pl.multiple_of(g * W, W), W)

    def load(src, dst, i):
        return pltpu.make_async_copy(src, dst, load_sem.at[i])

    def load_w(g, i):
        return pltpu.make_async_copy(
            (wq_hbm, wk_hbm, wv_hbm)[i].at[:, cols_of(g)], w_ref.at[i, g], w_sem.at[g, i]
        )

    def remote(src, dst, sem, at, to):
        return pltpu.make_async_remote_copy(
            src_ref=src, dst_ref=dst, send_sem=sem.at[(0, *at)], recv_sem=sem.at[(1, *at)],
            device_id=to, device_id_type=MESH,
        )

    barrier = pltpu.get_barrier_semaphore()
    peers = [sibling, across] + [*near.values()]
    def load_x(r):
        rows = slice(r * 256, (r + 1) * 256)
        return load(x_hbm.at[rows], x_ref.at[rows], 3 + r)

    load_x(0).start()
    for i in (1, 2):
        load_w(0, i).start()
    for r in (3, 1, 2):
        load_x(r).start()
    load(h_hbm, h_ref, 1).start()
    load_w(0, 0).start()
    for to in peers:
        pl.semaphore_signal(barrier, inc=1, device_id=to, device_id_type=MESH)
    pl.semaphore_wait(barrier, len(peers))

    def adjoint(g):
        return remote(a_hbm.at[:, cols_of(g)], adj_ref.at[g], adj_sem, (g,), near[0, 3])

    adjoint(0).start()

    def halo(g, side):
        return remote(kv_out.at[g, side], kv_in.at[g, 1 - side], kv_sem, (g, side), (down, up)[side])

    def project_kv(g, i, r):
        own = nn(x_ref[r * 256:(r + 1) * 256], w_ref[i, g]).astype(BF16)
        (k_ref, v_ref)[i - 1][g % 2, 1 + 2 * r:3 + 2 * r] = own.reshape(2, 128, W)
        if r == 0:
            kv_out[g, 0, i - 1] = own[:128]
        if r == 3:
            kv_out[g, 1, i - 1] = own[128:]

    def project_q(g):
        load_w(g, 0).wait()
        for r in range(2):
            rows = slice(r * 256, (r + 1) * 256)
            q_ref[g % 2, rows] = nn(h_ref[rows], w_ref[0, g]).astype(BF16) * 0.125

    def points(side):
        rows = pl.ds(896 * side, 128)
        return remote(x_hbm.at[rows], xh_ref.at[1 - side], xh_sem, (side,), (down, up)[side])

    def send_halos(g):
        for side in range(2):
            halo(g, side).start()

    def project(g):
        for i in (1, 2):
            load_w(g, i).wait()
            for r in range(4):
                project_kv(g, i, r)
        send_halos(g)
        project_q(g)

    for r in (0, 3, 1, 2):
        load_x(r).wait()
        for i in (1, 2):
            if r == 0:
                load_w(0, i).wait()
            project_kv(0, i, r)
        rows = slice(r * 256, (r + 1) * 256)
        xt_ref[:, rows] = x_ref[rows].T
        if r == 3:
            send_halos(0)
            load(mask_hbm, mask_ref, 2).start()
            for g in range(1, GROUPS):
                for i in range(3):
                    load_w(g, i).start()
    load(h_hbm, h_ref, 1).wait()
    project_q(0)
    for r in range(2):
        rows = slice(r * 256, (r + 1) * 256)
        ht_ref[:, rows] = h_ref[rows].T

    load(mask_hbm, mask_ref, 2).wait()

    @pl.loop(0, 4)
    def _(m):
        for s in range(4):
            bias_ref[m, s * 128:(s + 1) * 128, :] = (mask_ref[m * 4 + s].astype(F32).T - 1.0) * 1e30

    dk_part[16] = jnp.zeros((128, 128), F32)
    dv_part[16] = jnp.zeros((128, 128), F32)

    for e in range(16):
        local_ref[e] = jnp.clip(ids_ref[e] - band * 8 + 1, 0, 9)
    for block in range(10):
        for m in range(4):
            at = 16
            for s in range(4):
                off = local_ref[m * 4 + s] - block
                at = at + (1 - jnp.minimum(off * off, 1)) * (m * 4 + s - 16)
            lists_ref[block * 4 + m] = jnp.clip(at, 0, 16)

    def operands(g, pair, m):
        turn = g % 2
        rows = slice(m * 128, (m + 1) * 128)
        cols = pl.ds(pl.multiple_of(pair * 128, 128), 128)
        blocks = [local_ref[m * 4 + s] for s in range(4)]
        keys = jnp.concatenate([k_ref[turn, b, :, cols] for b in blocks], axis=0)
        values = jnp.concatenate([v_ref[turn, b, :, cols] for b in blocks], axis=0)
        qq = paired(q_ref[turn, rows, cols])
        aa = paired(adj_ref[g, rows, cols])
        return keys, qq, aa, nt(keys, qq), nt(values, aa)

    def weigh(m, scores, dprobs):
        bias = bias_ref[m]
        bias = jnp.concatenate([bias, bias], axis=1)
        scores = scores + bias
        top = jnp.max(scores, axis=0, keepdims=True)
        expo = jnp.exp(scores - top)
        probs = expo * (1.0 / jnp.sum(expo, axis=0, keepdims=True))
        probs_b = probs.astype(BF16)
        delta = jnp.sum(probs_b.astype(F32) * dprobs, axis=0, keepdims=True)
        return probs_b, (probs * (dprobs - delta)).astype(BF16)

    def spread(g, pair, m, keys, qq, aa, probs_b, ds):
        rows = slice(m * 128, (m + 1) * 128)
        cols = pl.ds(pl.multiple_of(pair * 128, 128), 128)
        dv = nn(probs_b, aa)
        dk = nn(ds, qq)
        for s in range(4):
            dv_part[m * 4 + s] = dv[s * 128:(s + 1) * 128]
            dk_part[m * 4 + s] = dk[s * 128:(s + 1) * 128]
        dq = tn(keys, ds)
        dq = jnp.concatenate([dq[:64, :128], dq[64:, 128:]], axis=0) * 0.125
        dq_ref[g, rows, cols] = dq.T.astype(BF16)

    def gathered(part, block):
        found = [part[lists_ref[block * 4 + m]] for m in range(4)]
        return (found[0] + found[1]) + (found[2] + found[3])

    def attend_pair(g, pair):
        cols = pl.ds(pl.multiple_of(pair * 128, 128), 128)
        ready = operands(g, pair, 0)
        done = None
        for m in range(4):
            keys, qq, aa, scores, dprobs = ready
            if m < 3:
                ready = operands(g, pair, m + 1)
            weighed = weigh(m, scores, dprobs)
            if done is not None:
                spread(g, pair, m - 1, *done)
            done = (keys, qq, aa, *weighed)
        spread(g, pair, 3, *done)
        for i, part in enumerate((dk_part, dv_part)):
            dkv_out[g, 0, i, :, cols] = gathered(part, 0).astype(BF16)
            dkv_out[g, 1, i, :, cols] = gathered(part, 9).astype(BF16)
            edge_ref[g % 2, 0, i, :, cols] = gathered(part, 1)
            edge_ref[g % 2, 1, i, :, cols] = gathered(part, 8)

        @pl.when(pair == PAIRS - 1)
        def _():
            for side in range(2):
                back(g, side).start()

        @pl.loop(1, 7)
        def _(block):
            rows = pl.ds(pl.multiple_of(block * 128, 128), 128)
            dk_ref[g, rows, cols] = gathered(dk_part, block + 1).astype(BF16)
            dv_ref[g, rows, cols] = gathered(dv_part, block + 1).astype(BF16)

    def back(g, side):
        return remote(dkv_out.at[g, side], dkv_in.at[g, 1 - side], dkv_sem, (g, side), (down, up)[side])

    def merge(g):
        for side in range(2):
            back(g, side).wait()
        for i, ref in enumerate((dk_ref, dv_ref)):
            ref[g, 0:128, :] = (edge_ref[g % 2, 0, i] + dkv_in[g, 0, i].astype(F32)).astype(BF16)
            ref[g, 896:1024, :] = (edge_ref[g % 2, 1, i] + dkv_in[g, 1, i].astype(F32)).astype(BF16)

    def swap(g):
        return remote(term_ref.at[g, 1 - core], core_in.at[g], core_sem, (g,), sibling)

    def terms(g, which=(0, 1, 2), outside=False):
        for t in which:
            strides = [(0, 64, 16)[axis] for axis in ORDERS[t]]
            for z in range(4):
                rows = slice(z * 256, (z + 1) * 256)
                if t == 0:
                    term = nn(ht_ref[rows], dq_ref[g])
                else:
                    term = nn(xt_ref[rows], (dk_ref, dv_ref)[t - 1][g])
                    if outside:
                        beyond = jnp.concatenate([dkv_out[g, 0, t - 1], dkv_out[g, 1, t - 1]], axis=0)
                        term = term + nn(xht_ref[rows], beyond)
                for c in range(2):
                    for n in range(0, 64, 2):
                        at = (n // 16, n // 4 % 4, n % 4)
                        if at[ORDERS[t].index(0)] != z:
                            continue
                        row = sum(a * b for a, b in zip(at, strides)) + c * 8
                        pieces = [term[row:row + 8], term[row + strides[2]:row + strides[2] + 8]]
                        term_ref[g, c, t, n * 8:n * 8 + 16, :] = jnp.concatenate(pieces, axis=0).astype(BF16)

    stages = ((a_out, a_in, a_sem, 128), (b_out, b_in, b_sem, 32), (c_out, c_in, c_sem, 8))

    bundles = (((0, 1), (1, 2), (2, 3)), ((0, 1), (1, 3)), ((0, 2), (2, 3)))

    def pass_on(g, level, bundle, steps):
        out, inside, sem, rows = stages[level]
        axis = ORDERS[bundle[0]][level]
        both = pl.ds(bundle[0], bundle[1] - bundle[0])
        first = pl.multiple_of(ahead[axis, steps] * rows, rows)
        return remote(
            out.at[g, both, pl.ds(first, rows), :], inside.at[g, steps - 1, both], sem, (g,), near[axis, steps]
        )

    def scatter(g, level, which=(0, 1, 2)):
        for steps in (2, 1, 3):
            for n, bundle in enumerate(bundles[level]):
                if n in which:
                    pass_on(g, level, bundle, steps).start()

    def arrived(g, level):
        _, inside, sem, _ = stages[level]
        for i in range(2):
            pltpu.make_async_copy(inside.at[g], inside.at[g], sem.at[i, g]).wait()

    def collected(g, level, t):
        out, inside, sem, rows = stages[level]
        own = pl.ds(pl.multiple_of(place[ORDERS[t][level]] * rows, rows), rows)
        total = out[g, t, own, :].astype(F32)
        for steps in (1, 2, 3):
            total = total + inside[g, steps - 1, t].astype(F32)
        return total

    def join_core(g, t):
        a_out[g, t] = (term_ref[g, core, t].astype(F32) + core_in[g, t].astype(F32)).astype(BF16)

    def reduce_core(g):
        swap(g).wait()
        for t in range(3):
            join_core(g, t)
        scatter(g, 0)

    def swap_one(t):
        return remote(
            term_ref.at[GROUPS - 1, 1 - core, t], core_in.at[GROUPS - 1, t], core_sem, (GROUPS - 1 + t,), sibling
        )

    def reduce_core_one(t):
        swap_one(t).wait()
        join_core(GROUPS - 1, t)
        scatter(GROUPS - 1, 0, (t,))

    def reduce_a(g):
        arrived(g, 0)
        for t in range(3):
            b_out[g, t] = collected(g, 0, t).astype(BF16)
        scatter(g, 1)

    def reduce_b(g):
        arrived(g, 1)
        for t in range(3):
            c_out[g, t] = collected(g, 1, t)
        scatter(g, 2)

    def reduce_c(g):
        arrived(g, 2)
        for t in range(3):
            wg_ref[:, pl.ds(pl.multiple_of(t * D + g * W, W), W)] = collected(g, 2, t) * 0.25

    @pl.loop(0, GROUPS)
    def _(g):
        @pl.when(g < GROUPS - 1)
        def _():
            project(g + 1)

        adjoint(g).wait()

        @pl.when(g < GROUPS - 1)
        def _():
            adjoint(g + 1).start()

        for side in range(2):
            halo(g, side).wait()
        @pl.when(g == 0)
        def _():
            for side in range(2):
                points(side).start()

        @pl.when(g == GROUPS - 2)
        def _():
            for side in range(2):
                points(side).wait()
            for side in range(2):
                xht_ref[:, side * 128:(side + 1) * 128] = xh_ref[side].T

        turn = g % 2
        for i, ref in enumerate((k_ref, v_ref)):
            ref[turn, 0] = kv_in[g, 0, i]
            ref[turn, 9] = kv_in[g, 1, i]

        @pl.loop(0, PAIRS)
        def _(pair):
            @pl.when((pair == 1) & (g > 2))
            def _():
                reduce_c(g - 3)

            @pl.when((pair == 1) & (g > 1))
            def _():
                reduce_a(g - 2)

            @pl.when((pair == 1) & (g > 0))
            def _():
                merge(g - 1)
                terms(g - 1)
                swap(g - 1).start()

            attend_pair(g, pair)

        @pl.when(g > 1)
        def _():
            reduce_b(g - 2)

        @pl.when(g > 0)
        def _():
            reduce_core(g - 1)

    last = GROUPS - 1
    for i, ref in enumerate((dk_ref, dv_ref)):
        ref[last, 0:128, :] = edge_ref[last % 2, 0, i].astype(BF16)
        ref[last, 896:1024, :] = edge_ref[last % 2, 1, i].astype(BF16)
    for t in range(3):
        terms(last, (t,), t > 0)
        swap_one(t).start()
    for r in range(2):
        rows = slice(r * 256, (r + 1) * 256)
        for n in range(4):
            cols = slice(n * 256, (n + 1) * 256)
            total = None
            for g in range(GROUPS):
                part = nt(dq_ref[g, rows], w_ref[0, g, cols])
                total = part if total is None else total + part
            mg_ref[rows, cols] = total.astype(BF16)
    pltpu.make_async_copy(mg_ref, mg_hbm, out_sem.at[0]).start()

    def grid_grads(n):
        cols = slice(n * 256, (n + 1) * 256)
        for r in range(4):
            rows = slice(r * 256, (r + 1) * 256)
            total = None
            for g in range(GROUPS):
                for i, ref in enumerate((dk_ref, dv_ref)):
                    part = nt(ref[g, rows], w_ref[1 + i, g, cols])
                    total = part if total is None else total + part
            gg_ref[rows, cols] = total.astype(BF16)
        grid_out(n).start()

    def grid_out(n):
        return pltpu.make_async_copy(
            gg_ref.at[:, n * 256:(n + 1) * 256], gg_hbm.at[:, n * 256:(n + 1) * 256], out_sem.at[1 + n]
        )

    reduce_core_one(0)
    reduce_core_one(1)
    merge(last)
    reduce_core_one(2)
    reduce_a(last - 1)
    grid_grads(0)
    grid_grads(1)
    reduce_c(last - 2)
    reduce_b(last - 1)
    grid_grads(2)
    grid_grads(3)
    reduce_a(last)
    reduce_c(last - 1)
    reduce_b(last)
    reduce_c(last)
    copy = pltpu.make_async_copy(wg_ref, wg_hbm, out_sem.at[5])
    copy.start()
    copy.wait()
    pltpu.make_async_copy(mg_ref, mg_hbm, out_sem.at[0]).wait()
    for n in range(4):
        grid_out(n).wait()


def hand_out(gg, mg, wg, gg_out, mg_out, wg_out, gg_ref, mg_ref, wg_ref, sem):
    steps = []
    for src, held, dst, parts in ((gg, gg_ref, gg_out, 4), (mg, mg_ref, mg_out, 2), (wg, wg_ref, wg_out, 1)):
        rows = src.shape[0] // parts
        for part in range(parts):
            at = pl.ds(part * rows, rows)
            n = len(steps)
            steps.append((
                pltpu.make_async_copy(src.at[at], held.at[at], sem.at[0, n]),
                pltpu.make_async_copy(held.at[at], dst.at[at], sem.at[1, n]),
            ))
    for come, _ in steps:
        come.start()
    for come, go in steps:
        come.wait()
        go.start()
    for _, go in steps:
        go.wait()


def on_device(grid_feat, mesh_feat, mesh_adjoint, w_query, w_key, w_value, block_grid, block_mask):
    anywhere = pl.BlockSpec(memory_space=pl.ANY)
    dma = pltpu.SemaphoreType.DMA
    grid_grad, mesh_grad, w_grad = pl.pallas_call(
        kernel,
        in_specs=[pl.BlockSpec(memory_space=pltpu.SMEM)] + [anywhere] * 7,
        out_specs=[anywhere] * 3,
        out_shape=[
            jax.ShapeDtypeStruct((1024, D), BF16),
            jax.ShapeDtypeStruct((512, D), BF16),
            jax.ShapeDtypeStruct((8, 3 * D), F32),
        ],
        scratch_shapes=[
            pltpu.VMEM((1024, D), BF16),
            pltpu.VMEM((512, D), BF16),
            pltpu.VMEM((D, 1024), BF16),
            pltpu.VMEM((D, 512), BF16),
            pltpu.VMEM((3, GROUPS, D, W), BF16),
            pltpu.VMEM((16, 128, 128), jnp.int32),
            pltpu.VMEM((4, 512, 128), F32),
            pltpu.VMEM((GROUPS, 512, W), BF16),
            pltpu.VMEM((2, 512, W), BF16),
            pltpu.VMEM((2, 10, 128, W), BF16),
            pltpu.VMEM((2, 10, 128, W), BF16),
            pltpu.VMEM((GROUPS, 512, W), BF16),
            pltpu.VMEM((GROUPS, 1024, W), BF16),
            pltpu.VMEM((GROUPS, 1024, W), BF16),
            pltpu.VMEM((17, 128, 128), F32),
            pltpu.VMEM((17, 128, 128), F32),
            pltpu.VMEM((2, 2, 2, 128, W), F32),
            pltpu.VMEM((GROUPS, 2, 2, 128, W), BF16),
            pltpu.VMEM((GROUPS, 2, 2, 128, W), BF16),
            pltpu.VMEM((GROUPS, 2, 2, 128, W), BF16),
            pltpu.VMEM((GROUPS, 2, 2, 128, W), BF16),
            pltpu.VMEM((GROUPS, 2, 3, 512, W), BF16),
            pltpu.VMEM((GROUPS, 3, 512, W), BF16),
            pltpu.VMEM((GROUPS, 3, 512, W), BF16),
            pltpu.VMEM((GROUPS, 3, 3, 128, W), BF16),
            pltpu.VMEM((GROUPS, 3, 128, W), BF16),
            pltpu.VMEM((GROUPS, 3, 3, 32, W), BF16),
            pltpu.VMEM((GROUPS, 3, 32, W), F32),
            pltpu.VMEM((GROUPS, 3, 3, 8, W), F32),
            pltpu.VMEM((8, 3 * D), F32),
            pltpu.VMEM((1024, D), BF16),
            pltpu.VMEM((512, D), BF16),
            pltpu.VMEM((2, 128, D), BF16),
            pltpu.VMEM((D, 256), BF16),
            dma((2, 2)),
            pltpu.SMEM((16,), jnp.int32),
            pltpu.SMEM((40,), jnp.int32),
            dma((7,)),
            dma((GROUPS, 3)),
            dma((6,)),
            dma((2, GROUPS)),
            dma((2, GROUPS, 2)),
            dma((2, GROUPS, 2)),
            dma((2, GROUPS + 2)),
            dma((2, GROUPS)),
            dma((2, GROUPS)),
            dma((2, GROUPS)),
        ],
        compiler_params=pltpu.CompilerParams(
            collective_id=0, has_side_effects=True, vmem_limit_bytes=62 << 20
        ),
        cost_estimate=pl.CostEstimate(flops=20 * 2**30, bytes_accessed=20 << 20, transcendentals=4 << 20),
    )(block_grid, grid_feat[0], mesh_feat[0], mesh_adjoint[0], w_query, w_key, w_value, block_mask)
    results = (grid_grad, mesh_grad, w_grad)
    grid_grad, mesh_grad, w_grad = pl.pallas_call(
        hand_out,
        in_specs=[anywhere] * 3,
        out_specs=[anywhere] * 3,
        out_shape=[jax.ShapeDtypeStruct(r.shape, r.dtype) for r in results],
        scratch_shapes=[pltpu.VMEM(r.shape, r.dtype) for r in results] + [dma((2, 7))],
    )(*results)
    return (grid_grad[None], mesh_grad[None], w_grad)


def solution(mesh):
    placed = (
        P("sec", "space", None),
        P("sec", "space", None),
        P("sec", "space", None),
        P(),
        P(),
        P(),
        P("space"),
        P("space", None, None),
    )
    return jax.shard_map(
        on_device,
        mesh=mesh,
        in_specs=placed,
        out_specs=(P("sec", "space", None), P("sec", "space", None), P(("sec", "space"), None)),
        check_vma=False,
    )
```

```python
import jax
import jax.numpy as jnp
from jax import lax
from jax.experimental import pallas as pl
from jax.experimental.pallas import tpu as pltpu
from jax.sharding import PartitionSpec as P

F32, BF16 = jnp.float32, jnp.bfloat16
MESH = pl.DeviceIdType.MESH
D = 1024
GROUPS = 4
W = D // GROUPS
PAIRS = W // 128
BANDS = 32
ORDERS = ((0, 1, 2), (1, 0, 2), (2, 0, 1))


def nt(a, b):
    return lax.dot_general(a, b, (((1,), (1,)), ((), ())), preferred_element_type=F32)


def tn(a, b):
    return lax.dot_general(a, b, (((0,), (0,)), ((), ())), preferred_element_type=F32)


def nn(a, b):
    return lax.dot_general(a, b, (((1,), (0,)), ((), ())), preferred_element_type=F32)


def paired(x):
    left = lax.broadcasted_iota(jnp.int32, x.shape, 1) < 64
    zero = jnp.zeros_like(x)
    return jnp.concatenate([jnp.where(left, x, zero), jnp.where(left, zero, x)], axis=0)


def kernel(
    ids_ref, x_hbm, h_hbm, a_hbm, wq_hbm, wk_hbm, wv_hbm, mask_hbm,
    gg_hbm, mg_hbm, wg_hbm,
    x_ref, h_ref, xt_ref, ht_ref, w_ref, mask_ref, bias_ref, adj_ref, q_ref, k_ref, v_ref,
    dq_ref, dk_ref, dv_ref, dk_part, dv_part, edge_ref,
    kv_out, kv_in, dkv_out, dkv_in,
    term_ref, core_in, a_out, a_in, b_out, b_in, c_out, c_in, wg_ref, gg_ref, mg_ref,
    xh_ref, xht_ref, xh_sem, local_ref, lists_ref, load_sem, w_sem, out_sem, adj_sem, kv_sem, dkv_sem, core_sem, a_sem, b_sem, c_sem,
):
    sec = lax.axis_index("sec")
    band = lax.axis_index("space")
    core = band % 2
    gx = band // 8
    gy = (band // 2) % 4
    place = (sec, gx, gy)

    def space_of(x, y, c):
        return (x * 4 + y) * 2 + c

    def peer(axis, steps):
        z, x, y = place
        if axis == 0:
            return ((z + steps) % 4, band)
        if axis == 1:
            return (z, space_of((x + steps) % 4, y, core))
        return (z, space_of(x, (y + steps) % 4, core))

    near = {(axis, steps): peer(axis, steps) for axis in range(3) for steps in (1, 2, 3)}
    ahead = {(axis, steps): (place[axis] + steps) % 4 for axis in range(3) for steps in (1, 2, 3)}
    sibling = (sec, space_of(gx, gy, 1 - core))
    up = (sec, (band + 1) % BANDS)
    down = (sec, (band + BANDS - 1) % BANDS)
    across = (sec, (band + BANDS + 2 * core - 1) % BANDS)

    def cols_of(g):
        return pl.ds(pl.multiple_of(g * W, W), W)

    def load(src, dst, i):
        return pltpu.make_async_copy(src, dst, load_sem.at[i])

    def load_w(g, i):
        return pltpu.make_async_copy(
            (wq_hbm, wk_hbm, wv_hbm)[i].at[:, cols_of(g)], w_ref.at[i, g], w_sem.at[g, i]
        )

    def remote(src, dst, sem, at, to):
        return pltpu.make_async_remote_copy(
            src_ref=src, dst_ref=dst, send_sem=sem.at[(0, *at)], recv_sem=sem.at[(1, *at)],
            device_id=to, device_id_type=MESH,
        )

    barrier = pltpu.get_barrier_semaphore()
    peers = [sibling, across] + [*near.values()]
    def load_x(r):
        rows = slice(r * 256, (r + 1) * 256)
        return load(x_hbm.at[rows], x_ref.at[rows], 3 + r)

    load_x(0).start()
    for i in (1, 2):
        load_w(0, i).start()
    for r in (3, 1, 2):
        load_x(r).start()
    load(h_hbm, h_ref, 1).start()
    load_w(0, 0).start()
    for to in peers:
        pl.semaphore_signal(barrier, inc=1, device_id=to, device_id_type=MESH)
    pl.semaphore_wait(barrier, len(peers))

    def adjoint(g):
        return remote(a_hbm.at[:, cols_of(g)], adj_ref.at[g], adj_sem, (g,), near[0, 3])

    adjoint(0).start()

    for e in range(16):
        local_ref[e] = jnp.clip(ids_ref[e] - band * 8 + 1, 0, 9)
    for block in range(10):
        for m in range(4):
            at = 16
            for s in range(4):
                off = local_ref[m * 4 + s] - block
                at = at + (1 - jnp.minimum(off * off, 1)) * (m * 4 + s - 16)
            lists_ref[block * 4 + m] = jnp.clip(at, 0, 16)

    def halo(g, side):
        return remote(kv_out.at[g, side], kv_in.at[g, 1 - side], kv_sem, (g, side), (down, up)[side])

    def project_kv(g, i, r):
        own = nn(x_ref[r * 256:(r + 1) * 256], w_ref[i, g]).astype(BF16)
        (k_ref, v_ref)[i - 1][g % 2, 1 + 2 * r:3 + 2 * r] = own.reshape(2, 128, W)
        if r == 0:
            kv_out[g, 0, i - 1] = own[:128]
        if r == 3:
            kv_out[g, 1, i - 1] = own[128:]

    def project_q(g):
        load_w(g, 0).wait()
        for r in range(2):
            rows = slice(r * 256, (r + 1) * 256)
            q_ref[g % 2, rows] = nn(h_ref[rows], w_ref[0, g]).astype(BF16) * 0.125

    def points(side):
        rows = pl.ds(896 * side, 128)
        return remote(x_hbm.at[rows], xh_ref.at[1 - side], xh_sem, (side,), (down, up)[side])

    def send_halos(g):
        for side in range(2):
            halo(g, side).start()

    def project(g):
        for i in (1, 2):
            load_w(g, i).wait()
            for r in range(4):
                project_kv(g, i, r)
        send_halos(g)
        project_q(g)

    for r in (0, 3, 1, 2):
        load_x(r).wait()
        for i in (1, 2):
            if r == 0:
                load_w(0, i).wait()
            project_kv(0, i, r)
        rows = slice(r * 256, (r + 1) * 256)
        xt_ref[:, rows] = x_ref[rows].T
        if r == 3:
            send_halos(0)
            load(mask_hbm, mask_ref, 2).start()
            for g in range(1, GROUPS):
                for i in range(3):
                    load_w(g, i).start()
    load(h_hbm, h_ref, 1).wait()
    project_q(0)
    for r in range(2):
        rows = slice(r * 256, (r + 1) * 256)
        ht_ref[:, rows] = h_ref[rows].T

    load(mask_hbm, mask_ref, 2).wait()

    @pl.loop(0, 4)
    def _(m):
        for s in range(4):
            bias_ref[m, s * 128:(s + 1) * 128, :] = (mask_ref[m * 4 + s].astype(F32).T - 1.0) * 1e30

    dk_part[16] = jnp.zeros((128, 128), F32)
    dv_part[16] = jnp.zeros((128, 128), F32)


    def operands(g, pair, m):
        turn = g % 2
        rows = slice(m * 128, (m + 1) * 128)
        cols = pl.ds(pl.multiple_of(pair * 128, 128), 128)
        blocks = [local_ref[m * 4 + s] for s in range(4)]
        keys = jnp.concatenate([k_ref[turn, b, :, cols] for b in blocks], axis=0)
        values = jnp.concatenate([v_ref[turn, b, :, cols] for b in blocks], axis=0)
        qq = paired(q_ref[turn, rows, cols])
        aa = paired(adj_ref[g, rows, cols])
        return keys, qq, aa, nt(keys, qq), nt(values, aa)

    def weigh(m, scores, dprobs):
        bias = bias_ref[m]
        bias = jnp.concatenate([bias, bias], axis=1)
        scores = scores + bias
        top = jnp.max(scores, axis=0, keepdims=True)
        expo = jnp.exp(scores - top)
        probs = expo * (1.0 / jnp.sum(expo, axis=0, keepdims=True))
        probs_b = probs.astype(BF16)
        delta = jnp.sum(probs_b.astype(F32) * dprobs, axis=0, keepdims=True)
        return probs_b, (probs * (dprobs - delta)).astype(BF16)

    def spread(g, pair, m, keys, qq, aa, probs_b, ds):
        rows = slice(m * 128, (m + 1) * 128)
        cols = pl.ds(pl.multiple_of(pair * 128, 128), 128)
        dv = nn(probs_b, aa)
        dk = nn(ds, qq)
        for s in range(4):
            dv_part[m * 4 + s] = dv[s * 128:(s + 1) * 128]
            dk_part[m * 4 + s] = dk[s * 128:(s + 1) * 128]
        dq = tn(keys, ds)
        dq = jnp.concatenate([dq[:64, :128], dq[64:, 128:]], axis=0) * 0.125
        dq_ref[g, rows, cols] = dq.T.astype(BF16)

    def gathered(part, block):
        found = [part[lists_ref[block * 4 + m]] for m in range(4)]
        return (found[0] + found[1]) + (found[2] + found[3])

    def attend_pair(g, pair):
        cols = pl.ds(pl.multiple_of(pair * 128, 128), 128)
        ready = operands(g, pair, 0)
        done = None
        for m in range(4):
            keys, qq, aa, scores, dprobs = ready
            if m < 3:
                ready = operands(g, pair, m + 1)
            weighed = weigh(m, scores, dprobs)
            if done is not None:
                spread(g, pair, m - 1, *done)
            done = (keys, qq, aa, *weighed)
        spread(g, pair, 3, *done)
        for i, part in enumerate((dk_part, dv_part)):
            dkv_out[g, 0, i, :, cols] = gathered(part, 0).astype(BF16)
            dkv_out[g, 1, i, :, cols] = gathered(part, 9).astype(BF16)
            edge_ref[g % 2, 0, i, :, cols] = gathered(part, 1)
            edge_ref[g % 2, 1, i, :, cols] = gathered(part, 8)

        @pl.when(pair == PAIRS - 1)
        def _():
            for side in range(2):
                back(g, side).start()

        @pl.loop(1, 7)
        def _(block):
            rows = pl.ds(pl.multiple_of(block * 128, 128), 128)
            dk_ref[g, rows, cols] = gathered(dk_part, block + 1).astype(BF16)
            dv_ref[g, rows, cols] = gathered(dv_part, block + 1).astype(BF16)

    def back(g, side):
        return remote(dkv_out.at[g, side], dkv_in.at[g, 1 - side], dkv_sem, (g, side), (down, up)[side])

    def merge(g):
        for side in range(2):
            back(g, side).wait()
        for i, ref in enumerate((dk_ref, dv_ref)):
            ref[g, 0:128, :] = (edge_ref[g % 2, 0, i] + dkv_in[g, 0, i].astype(F32)).astype(BF16)
            ref[g, 896:1024, :] = (edge_ref[g % 2, 1, i] + dkv_in[g, 1, i].astype(F32)).astype(BF16)

    def swap(g, t):
        return remote(term_ref.at[g, 1 - core, t], core_in.at[g, t], core_sem, (g, t), sibling)

    def terms(g, which=(0, 1, 2), outside=False):
        for t in which:
            strides = [(0, 64, 16)[axis] for axis in ORDERS[t]]
            for z in range(4):
                rows = slice(z * 256, (z + 1) * 256)
                if t == 0:
                    term = nn(ht_ref[rows], dq_ref[g])
                else:
                    term = nn(xt_ref[rows], (dk_ref, dv_ref)[t - 1][g])
                    if outside:
                        beyond = jnp.concatenate([dkv_out[g, 0, t - 1], dkv_out[g, 1, t - 1]], axis=0)
                        term = term + nn(xht_ref[rows], beyond)
                for c in range(2):
                    for n in range(0, 64, 2):
                        at = (n // 16, n // 4 % 4, n % 4)
                        if at[ORDERS[t].index(0)] != z:
                            continue
                        row = sum(a * b for a, b in zip(at, strides)) + c * 8
                        pieces = [term[row:row + 8], term[row + strides[2]:row + strides[2] + 8]]
                        term_ref[g, c, t, n * 8:n * 8 + 16, :] = jnp.concatenate(pieces, axis=0).astype(BF16)

    stages = ((a_out, a_in, a_sem, 128), (b_out, b_in, b_sem, 32), (c_out, c_in, c_sem, 8))

    bundles = (((0, 1), (1, 2), (2, 3)), ((0, 1), (1, 3)), ((0, 2), (2, 3)))

    def pass_on(g, level, bundle, steps):
        out, inside, sem, rows = stages[level]
        axis = ORDERS[bundle[0]][level]
        both = pl.ds(bundle[0], bundle[1] - bundle[0])
        first = pl.multiple_of(ahead[axis, steps] * rows, rows)
        return remote(
            out.at[g, both, pl.ds(first, rows), :], inside.at[g, steps - 1, both], sem, (g,), near[axis, steps]
        )

    def scatter(g, level, which=(0, 1, 2)):
        for steps in (2, 1, 3):
            for n, bundle in enumerate(bundles[level]):
                if n in which:
                    pass_on(g, level, bundle, steps).start()

    def arrived(g, level):
        _, inside, sem, _ = stages[level]
        for i in range(2):
            pltpu.make_async_copy(inside.at[g], inside.at[g], sem.at[i, g]).wait()

    def collected(g, level, t):
        out, inside, sem, rows = stages[level]
        own = pl.ds(pl.multiple_of(place[ORDERS[t][level]] * rows, rows), rows)
        total = out[g, t, own, :].astype(F32)
        for steps in (1, 2, 3):
            total = total + inside[g, steps - 1, t].astype(F32)
        return total

    def join_core(g, t):
        a_out[g, t] = (term_ref[g, core, t].astype(F32) + core_in[g, t].astype(F32)).astype(BF16)

    def reduce_core(g, which=(0, 1, 2)):
        for t in which:
            swap(g, t).wait()
            join_core(g, t)
        scatter(g, 0, which)

    def reduce_a(g):
        arrived(g, 0)
        for t in range(3):
            b_out[g, t] = collected(g, 0, t).astype(BF16)
        scatter(g, 1)

    def reduce_b(g):
        arrived(g, 1)
        for t in range(3):
            c_out[g, t] = collected(g, 1, t)
        scatter(g, 2)

    def reduce_c(g):
        arrived(g, 2)
        for t in range(3):
            wg_ref[:, pl.ds(pl.multiple_of(t * D + g * W, W), W)] = collected(g, 2, t) * 0.25

    @pl.loop(0, GROUPS)
    def _(g):
        @pl.when(g < GROUPS - 1)
        def _():
            project(g + 1)

        adjoint(g).wait()

        @pl.when(g < GROUPS - 1)
        def _():
            adjoint(g + 1).start()

        for side in range(2):
            halo(g, side).wait()
        @pl.when(g == 0)
        def _():
            for side in range(2):
                points(side).start()

        @pl.when(g == GROUPS - 2)
        def _():
            for side in range(2):
                points(side).wait()
            for side in range(2):
                xht_ref[:, side * 128:(side + 1) * 128] = xh_ref[side].T

        turn = g % 2
        for i, ref in enumerate((k_ref, v_ref)):
            ref[turn, 0] = kv_in[g, 0, i]
            ref[turn, 9] = kv_in[g, 1, i]

        @pl.loop(0, PAIRS)
        def _(pair):
            @pl.when((pair == 1) & (g > 0))
            def _():
                merge(g - 1)
                for t in range(3):
                    terms(g - 1, (t,))
                    swap(g - 1, t).start()

            @pl.when((pair == 1) & (g > 1))
            def _():
                reduce_a(g - 2)

            @pl.when((pair == 1) & (g > 2))
            def _():
                reduce_c(g - 3)

            attend_pair(g, pair)

        @pl.when(g > 1)
        def _():
            reduce_b(g - 2)

        @pl.when(g > 0)
        def _():
            reduce_core(g - 1)

    last = GROUPS - 1
    for i, ref in enumerate((dk_ref, dv_ref)):
        ref[last, 0:128, :] = edge_ref[last % 2, 0, i].astype(BF16)
        ref[last, 896:1024, :] = edge_ref[last % 2, 1, i].astype(BF16)
    for t in range(3):
        terms(last, (t,), t > 0)
        swap(last, t).start()
    for r in range(2):
        rows = slice(r * 256, (r + 1) * 256)
        for n in range(4):
            cols = slice(n * 256, (n + 1) * 256)
            total = None
            for g in range(GROUPS):
                part = nt(dq_ref[g, rows], w_ref[0, g, cols])
                total = part if total is None else total + part
            mg_ref[rows, cols] = total.astype(BF16)
    pltpu.make_async_copy(mg_ref, mg_hbm, out_sem.at[0]).start()

    def grid_grads(n):
        cols = slice(n * 256, (n + 1) * 256)
        for r in range(4):
            rows = slice(r * 256, (r + 1) * 256)
            total = None
            for g in range(GROUPS):
                for i, ref in enumerate((dk_ref, dv_ref)):
                    part = nt(ref[g, rows], w_ref[1 + i, g, cols])
                    total = part if total is None else total + part
            gg_ref[rows, cols] = total.astype(BF16)
        grid_out(n).start()

    def grid_out(n):
        return pltpu.make_async_copy(
            gg_ref.at[:, n * 256:(n + 1) * 256], gg_hbm.at[:, n * 256:(n + 1) * 256], out_sem.at[1 + n]
        )

    reduce_core(last, (0,))
    reduce_core(last, (1,))
    merge(last)
    reduce_core(last, (2,))
    reduce_a(last - 1)
    grid_grads(0)
    grid_grads(1)
    reduce_c(last - 2)
    reduce_b(last - 1)
    grid_grads(2)
    grid_grads(3)
    reduce_a(last)
    reduce_c(last - 1)
    reduce_b(last)
    reduce_c(last)
    copy = pltpu.make_async_copy(wg_ref, wg_hbm, out_sem.at[5])
    copy.start()
    copy.wait()
    pltpu.make_async_copy(mg_ref, mg_hbm, out_sem.at[0]).wait()
    for n in range(4):
        grid_out(n).wait()


def hand_out(gg, mg, wg, gg_out, mg_out, wg_out, gg_ref, mg_ref, wg_ref, sem):
    steps = []
    for src, held, dst, parts in ((gg, gg_ref, gg_out, 4), (mg, mg_ref, mg_out, 2), (wg, wg_ref, wg_out, 1)):
        rows = src.shape[0] // parts
        for part in range(parts):
            at = pl.ds(part * rows, rows)
            n = len(steps)
            steps.append((
                pltpu.make_async_copy(src.at[at], held.at[at], sem.at[0, n]),
                pltpu.make_async_copy(held.at[at], dst.at[at], sem.at[1, n]),
            ))
    for come, _ in steps:
        come.start()
    for come, go in steps:
        come.wait()
        go.start()
    for _, go in steps:
        go.wait()


def on_device(grid_feat, mesh_feat, mesh_adjoint, w_query, w_key, w_value, block_grid, block_mask):
    anywhere = pl.BlockSpec(memory_space=pl.ANY)
    dma = pltpu.SemaphoreType.DMA
    grid_grad, mesh_grad, w_grad = pl.pallas_call(
        kernel,
        in_specs=[pl.BlockSpec(memory_space=pltpu.SMEM)] + [anywhere] * 7,
        out_specs=[anywhere] * 3,
        out_shape=[
            jax.ShapeDtypeStruct((1024, D), BF16),
            jax.ShapeDtypeStruct((512, D), BF16),
            jax.ShapeDtypeStruct((8, 3 * D), F32),
        ],
        scratch_shapes=[
            pltpu.VMEM((1024, D), BF16),
            pltpu.VMEM((512, D), BF16),
            pltpu.VMEM((D, 1024), BF16),
            pltpu.VMEM((D, 512), BF16),
            pltpu.VMEM((3, GROUPS, D, W), BF16),
            pltpu.VMEM((16, 128, 128), jnp.int32),
            pltpu.VMEM((4, 512, 128), F32),
            pltpu.VMEM((GROUPS, 512, W), BF16),
            pltpu.VMEM((2, 512, W), BF16),
            pltpu.VMEM((2, 10, 128, W), BF16),
            pltpu.VMEM((2, 10, 128, W), BF16),
            pltpu.VMEM((GROUPS, 512, W), BF16),
            pltpu.VMEM((GROUPS, 1024, W), BF16),
            pltpu.VMEM((GROUPS, 1024, W), BF16),
            pltpu.VMEM((17, 128, 128), F32),
            pltpu.VMEM((17, 128, 128), F32),
            pltpu.VMEM((2, 2, 2, 128, W), F32),
            pltpu.VMEM((GROUPS, 2, 2, 128, W), BF16),
            pltpu.VMEM((GROUPS, 2, 2, 128, W), BF16),
            pltpu.VMEM((GROUPS, 2, 2, 128, W), BF16),
            pltpu.VMEM((GROUPS, 2, 2, 128, W), BF16),
            pltpu.VMEM((GROUPS, 2, 3, 512, W), BF16),
            pltpu.VMEM((GROUPS, 3, 512, W), BF16),
            pltpu.VMEM((GROUPS, 3, 512, W), BF16),
            pltpu.VMEM((GROUPS, 3, 3, 128, W), BF16),
            pltpu.VMEM((GROUPS, 3, 128, W), BF16),
            pltpu.VMEM((GROUPS, 3, 3, 32, W), BF16),
            pltpu.VMEM((GROUPS, 3, 32, W), F32),
            pltpu.VMEM((GROUPS, 3, 3, 8, W), F32),
            pltpu.VMEM((8, 3 * D), F32),
            pltpu.VMEM((1024, D), BF16),
            pltpu.VMEM((512, D), BF16),
            pltpu.VMEM((2, 128, D), BF16),
            pltpu.VMEM((D, 256), BF16),
            dma((2, 2)),
            pltpu.SMEM((16,), jnp.int32),
            pltpu.SMEM((40,), jnp.int32),
            dma((7,)),
            dma((GROUPS, 3)),
            dma((6,)),
            dma((2, GROUPS)),
            dma((2, GROUPS, 2)),
            dma((2, GROUPS, 2)),
            dma((2, GROUPS, 3)),
            dma((2, GROUPS)),
            dma((2, GROUPS)),
            dma((2, GROUPS)),
        ],
        compiler_params=pltpu.CompilerParams(
            collective_id=0, has_side_effects=True, vmem_limit_bytes=62 << 20
        ),
        cost_estimate=pl.CostEstimate(flops=20 * 2**30, bytes_accessed=20 << 20, transcendentals=4 << 20),
    )(block_grid, grid_feat[0], mesh_feat[0], mesh_adjoint[0], w_query, w_key, w_value, block_mask)
    results = (grid_grad, mesh_grad, w_grad)
    grid_grad, mesh_grad, w_grad = pl.pallas_call(
        hand_out,
        in_specs=[anywhere] * 3,
        out_specs=[anywhere] * 3,
        out_shape=[jax.ShapeDtypeStruct(r.shape, r.dtype) for r in results],
        scratch_shapes=[pltpu.VMEM(r.shape, r.dtype) for r in results] + [dma((2, 7))],
    )(*results)
    return (grid_grad[None], mesh_grad[None], w_grad)


def solution(mesh):
    placed = (
        P("sec", "space", None),
        P("sec", "space", None),
        P("sec", "space", None),
        P(),
        P(),
        P(),
        P("space"),
        P("space", None, None),
    )
    return jax.shard_map(
        on_device,
        mesh=mesh,
        in_specs=placed,
        out_specs=(P("sec", "space", None), P("sec", "space", None), P(("sec", "space"), None)),
        check_vma=False,
    )
```

```python
import jax
import jax.numpy as jnp
from jax import lax
from jax.experimental import pallas as pl
from jax.experimental.pallas import tpu as pltpu
from jax.sharding import PartitionSpec as P

F32, BF16 = jnp.float32, jnp.bfloat16
MESH = pl.DeviceIdType.MESH
D = 1024
GROUPS = 4
W = D // GROUPS
PAIRS = W // 128
BANDS = 32
ORDERS = ((0, 1, 2), (1, 0, 2), (2, 0, 1))


def nt(a, b):
    return lax.dot_general(a, b, (((1,), (1,)), ((), ())), preferred_element_type=F32)


def tn(a, b):
    return lax.dot_general(a, b, (((0,), (0,)), ((), ())), preferred_element_type=F32)


def nn(a, b):
    return lax.dot_general(a, b, (((1,), (0,)), ((), ())), preferred_element_type=F32)


def paired(x):
    left = lax.broadcasted_iota(jnp.int32, x.shape, 1) < 64
    zero = jnp.zeros_like(x)
    return jnp.concatenate([jnp.where(left, x, zero), jnp.where(left, zero, x)], axis=0)


def kernel(
    ids_ref, x_hbm, h_hbm, a_hbm, wq_hbm, wk_hbm, wv_hbm, mask_hbm,
    gg_hbm, mg_hbm, wg_hbm,
    x_ref, h_ref, xt_ref, ht_ref, w_ref, mask_ref, bias_ref, adj_ref, q_ref, k_ref, v_ref,
    dq_ref, dk_ref, dv_ref, dk_part, dv_part, edge_ref,
    kv_out, kv_in, dkv_out, dkv_in,
    term_ref, core_in, a_out, a_in, b_out, b_in, c_out, c_in, wg_ref, gg_ref, mg_ref,
    xh_ref, xht_ref, xh_sem, local_ref, lists_ref, load_sem, w_sem, out_sem, adj_sem, kv_sem, dkv_sem, core_sem, a_sem, b_sem, c_sem,
):
    sec = lax.axis_index("sec")
    band = lax.axis_index("space")
    core = band % 2
    gx = band // 8
    gy = (band // 2) % 4
    place = (sec, gx, gy)

    def space_of(x, y, c):
        return (x * 4 + y) * 2 + c

    def peer(axis, steps):
        z, x, y = place
        if axis == 0:
            return ((z + steps) % 4, band)
        if axis == 1:
            return (z, space_of((x + steps) % 4, y, core))
        return (z, space_of(x, (y + steps) % 4, core))

    near = {(axis, steps): peer(axis, steps) for axis in range(3) for steps in (1, 2, 3)}
    ahead = {(axis, steps): (place[axis] + steps) % 4 for axis in range(3) for steps in (1, 2, 3)}
    sibling = (sec, space_of(gx, gy, 1 - core))
    up = (sec, (band + 1) % BANDS)
    down = (sec, (band + BANDS - 1) % BANDS)
    across = (sec, (band + BANDS + 2 * core - 1) % BANDS)

    def cols_of(g):
        return pl.ds(pl.multiple_of(g * W, W), W)

    def load(src, dst, i):
        return pltpu.make_async_copy(src, dst, load_sem.at[i])

    def load_w(g, i):
        return pltpu.make_async_copy(
            (wq_hbm, wk_hbm, wv_hbm)[i].at[:, cols_of(g)], w_ref.at[i, g], w_sem.at[g, i]
        )

    def remote(src, dst, sem, at, to):
        return pltpu.make_async_remote_copy(
            src_ref=src, dst_ref=dst, send_sem=sem.at[(0, *at)], recv_sem=sem.at[(1, *at)],
            device_id=to, device_id_type=MESH,
        )

    barrier = pltpu.get_barrier_semaphore()
    peers = [sibling, across] + [*near.values()]
    def load_x(r):
        rows = slice(r * 256, (r + 1) * 256)
        return load(x_hbm.at[rows], x_ref.at[rows], 3 + r)

    load_x(0).start()
    for i in (1, 2):
        load_w(0, i).start()
    for r in (3, 1, 2):
        load_x(r).start()
    load(h_hbm, h_ref, 1).start()
    load_w(0, 0).start()
    for to in peers:
        pl.semaphore_signal(barrier, inc=1, device_id=to, device_id_type=MESH)
    pl.semaphore_wait(barrier, len(peers))

    def adjoint(g):
        return remote(a_hbm.at[:, cols_of(g)], adj_ref.at[g], adj_sem, (g,), near[0, 3])

    adjoint(0).start()

    for e in range(16):
        local_ref[e] = jnp.clip(ids_ref[e] - band * 8 + 1, 0, 9)
    for block in range(10):
        for m in range(4):
            at = 16
            for s in range(4):
                off = local_ref[m * 4 + s] - block
                at = at + (1 - jnp.minimum(off * off, 1)) * (m * 4 + s - 16)
            lists_ref[block * 4 + m] = jnp.clip(at, 0, 16)

    def halo(g, side):
        return remote(kv_out.at[g, side], kv_in.at[g, 1 - side], kv_sem, (g, side), (down, up)[side])

    def project_kv(g, i, r):
        own = nn(x_ref[r * 256:(r + 1) * 256], w_ref[i, g]).astype(BF16)
        (k_ref, v_ref)[i - 1][g % 2, 1 + 2 * r:3 + 2 * r] = own.reshape(2, 128, W)
        if r == 0:
            kv_out[g, 0, i - 1] = own[:128]
        if r == 3:
            kv_out[g, 1, i - 1] = own[128:]

    def project_q(g):
        load_w(g, 0).wait()
        for r in range(2):
            rows = slice(r * 256, (r + 1) * 256)
            q_ref[g % 2, rows] = nn(h_ref[rows], w_ref[0, g]).astype(BF16) * 0.125

    def points(side):
        rows = pl.ds(896 * side, 128)
        return remote(x_hbm.at[rows], xh_ref.at[1 - side], xh_sem, (side,), (down, up)[side])

    def send_halos(g):
        for side in range(2):
            halo(g, side).start()

    def project(g):
        for i in (1, 2):
            load_w(g, i).wait()
            for r in range(4):
                project_kv(g, i, r)
        send_halos(g)
        project_q(g)

    for r in (0, 3, 1, 2):
        load_x(r).wait()
        for i in (1, 2):
            if r == 0:
                load_w(0, i).wait()
            project_kv(0, i, r)
        rows = slice(r * 256, (r + 1) * 256)
        xt_ref[:, rows] = x_ref[rows].T
        if r == 3:
            send_halos(0)
            load(mask_hbm, mask_ref, 2).start()
            for g in range(1, GROUPS):
                for i in range(3):
                    load_w(g, i).start()
    load(h_hbm, h_ref, 1).wait()
    project_q(0)
    for r in range(2):
        rows = slice(r * 256, (r + 1) * 256)
        ht_ref[:, rows] = h_ref[rows].T

    load(mask_hbm, mask_ref, 2).wait()

    @pl.loop(0, 4)
    def _(m):
        for s in range(4):
            bias_ref[m, s * 128:(s + 1) * 128, :] = (mask_ref[m * 4 + s].astype(F32).T - 1.0) * 1e30

    dk_part[16] = jnp.zeros((128, 128), F32)
    dv_part[16] = jnp.zeros((128, 128), F32)


    def operands(g, pair, m):
        turn = g % 2
        rows = slice(m * 128, (m + 1) * 128)
        cols = pl.ds(pl.multiple_of(pair * 128, 128), 128)
        blocks = [local_ref[m * 4 + s] for s in range(4)]
        keys = jnp.concatenate([k_ref[turn, b, :, cols] for b in blocks], axis=0)
        values = jnp.concatenate([v_ref[turn, b, :, cols] for b in blocks], axis=0)
        qq = paired(q_ref[turn, rows, cols])
        aa = paired(adj_ref[g, rows, cols])
        return keys, qq, aa, nt(keys, qq), nt(values, aa)

    def weigh(m, scores, dprobs):
        bias = bias_ref[m]
        bias = jnp.concatenate([bias, bias], axis=1)
        scores = scores + bias
        top = jnp.max(scores, axis=0, keepdims=True)
        expo = jnp.exp(scores - top)
        probs = expo * (1.0 / jnp.sum(expo, axis=0, keepdims=True))
        probs_b = probs.astype(BF16)
        delta = jnp.sum(probs_b.astype(F32) * dprobs, axis=0, keepdims=True)
        return probs_b, (probs * (dprobs - delta)).astype(BF16)

    def spread(g, pair, m, keys, qq, aa, probs_b, ds):
        rows = slice(m * 128, (m + 1) * 128)
        cols = pl.ds(pl.multiple_of(pair * 128, 128), 128)
        dv = nn(probs_b, aa)
        dk = nn(ds, qq)
        for s in range(4):
            dv_part[m * 4 + s] = dv[s * 128:(s + 1) * 128]
            dk_part[m * 4 + s] = dk[s * 128:(s + 1) * 128]
        dq = tn(keys, ds)
        dq = jnp.concatenate([dq[:64, :128], dq[64:, 128:]], axis=0) * 0.125
        dq_ref[g, rows, cols] = dq.T.astype(BF16)

    def gathered(part, block):
        found = [part[lists_ref[block * 4 + m]] for m in range(4)]
        return (found[0] + found[1]) + (found[2] + found[3])

    def attend_pair(g, pair):
        cols = pl.ds(pl.multiple_of(pair * 128, 128), 128)
        ready = operands(g, pair, 0)
        done = None
        for m in range(4):
            keys, qq, aa, scores, dprobs = ready
            if m < 3:
                ready = operands(g, pair, m + 1)
            weighed = weigh(m, scores, dprobs)
            if done is not None:
                spread(g, pair, m - 1, *done)
            done = (keys, qq, aa, *weighed)
        spread(g, pair, 3, *done)
        for i, part in enumerate((dk_part, dv_part)):
            dkv_out[g, 0, i, :, cols] = gathered(part, 0).astype(BF16)
            dkv_out[g, 1, i, :, cols] = gathered(part, 9).astype(BF16)
            edge_ref[g % 2, 0, i, :, cols] = gathered(part, 1)
            edge_ref[g % 2, 1, i, :, cols] = gathered(part, 8)

        @pl.when(pair == PAIRS - 1)
        def _():
            for side in range(2):
                back(g, side).start()

        for block in range(1, 7):
            rows = slice(block * 128, (block + 1) * 128)
            dk_ref[g, rows, cols] = gathered(dk_part, block + 1).astype(BF16)
            dv_ref[g, rows, cols] = gathered(dv_part, block + 1).astype(BF16)

    def back(g, side):
        return remote(dkv_out.at[g, side], dkv_in.at[g, 1 - side], dkv_sem, (g, side), (down, up)[side])

    def merge(g):
        for side in range(2):
            back(g, side).wait()
        for i, ref in enumerate((dk_ref, dv_ref)):
            ref[g, 0:128, :] = (edge_ref[g % 2, 0, i] + dkv_in[g, 0, i].astype(F32)).astype(BF16)
            ref[g, 896:1024, :] = (edge_ref[g % 2, 1, i] + dkv_in[g, 1, i].astype(F32)).astype(BF16)

    def swap(g, t):
        return remote(term_ref.at[g, 1 - core, t], core_in.at[g, t], core_sem, (g, t), sibling)

    def terms(g, which=(0, 1, 2), outside=False):
        for t in which:
            strides = [(0, 64, 16)[axis] for axis in ORDERS[t]]
            for z in range(4):
                rows = slice(z * 256, (z + 1) * 256)
                if t == 0:
                    term = nn(ht_ref[rows], dq_ref[g])
                else:
                    term = nn(xt_ref[rows], (dk_ref, dv_ref)[t - 1][g])
                    if outside:
                        beyond = jnp.concatenate([dkv_out[g, 0, t - 1], dkv_out[g, 1, t - 1]], axis=0)
                        term = term + nn(xht_ref[rows], beyond)
                for c in range(2):
                    for n in range(0, 64, 2):
                        at = (n // 16, n // 4 % 4, n % 4)
                        if at[ORDERS[t].index(0)] != z:
                            continue
                        row = sum(a * b for a, b in zip(at, strides)) + c * 8
                        pieces = [term[row:row + 8], term[row + strides[2]:row + strides[2] + 8]]
                        term_ref[g, c, t, n * 8:n * 8 + 16, :] = jnp.concatenate(pieces, axis=0).astype(BF16)

    stages = ((a_out, a_in, a_sem, 128), (b_out, b_in, b_sem, 32), (c_out, c_in, c_sem, 8))

    bundles = (((0, 1), (1, 2), (2, 3)), ((0, 1), (1, 3)), ((0, 2), (2, 3)))

    def pass_on(g, level, bundle, steps):
        out, inside, sem, rows = stages[level]
        axis = ORDERS[bundle[0]][level]
        both = pl.ds(bundle[0], bundle[1] - bundle[0])
        first = pl.multiple_of(ahead[axis, steps] * rows, rows)
        return remote(
            out.at[g, both, pl.ds(first, rows), :], inside.at[g, steps - 1, both], sem, (g,), near[axis, steps]
        )

    def scatter(g, level, which=(0, 1, 2)):
        for steps in (2, 1, 3):
            for n, bundle in enumerate(bundles[level]):
                if n in which:
                    pass_on(g, level, bundle, steps).start()

    def arrived(g, level):
        _, inside, sem, _ = stages[level]
        for i in range(2):
            pltpu.make_async_copy(inside.at[g], inside.at[g], sem.at[i, g]).wait()

    def collected(g, level, t):
        out, inside, sem, rows = stages[level]
        own = pl.ds(pl.multiple_of(place[ORDERS[t][level]] * rows, rows), rows)
        total = out[g, t, own, :].astype(F32)
        for steps in (1, 2, 3):
            total = total + inside[g, steps - 1, t].astype(F32)
        return total

    def join_core(g, t):
        a_out[g, t] = (term_ref[g, core, t].astype(F32) + core_in[g, t].astype(F32)).astype(BF16)

    def reduce_core(g, which=(0, 1, 2)):
        for t in which:
            swap(g, t).wait()
            join_core(g, t)
        scatter(g, 0, which)

    def reduce_a(g):
        arrived(g, 0)
        for t in range(3):
            b_out[g, t] = collected(g, 0, t).astype(BF16)
        scatter(g, 1)

    def reduce_b(g):
        arrived(g, 1)
        for t in range(3):
            c_out[g, t] = collected(g, 1, t)
        scatter(g, 2)

    def reduce_c(g):
        arrived(g, 2)
        for t in range(3):
            wg_ref[:, pl.ds(pl.multiple_of(t * D + g * W, W), W)] = collected(g, 2, t) * 0.25

    @pl.loop(0, GROUPS)
    def _(g):
        @pl.when(g < GROUPS - 1)
        def _():
            project(g + 1)

        adjoint(g).wait()

        @pl.when(g < GROUPS - 1)
        def _():
            adjoint(g + 1).start()

        for side in range(2):
            halo(g, side).wait()
        @pl.when(g == 0)
        def _():
            for side in range(2):
                points(side).start()

        @pl.when(g == GROUPS - 2)
        def _():
            for side in range(2):
                points(side).wait()
            for side in range(2):
                xht_ref[:, side * 128:(side + 1) * 128] = xh_ref[side].T

        turn = g % 2
        for i, ref in enumerate((k_ref, v_ref)):
            ref[turn, 0] = kv_in[g, 0, i]
            ref[turn, 9] = kv_in[g, 1, i]

        @pl.loop(0, PAIRS)
        def _(pair):
            @pl.when((pair == 1) & (g > 0))
            def _():
                merge(g - 1)
                for t in range(3):
                    terms(g - 1, (t,))
                    swap(g - 1, t).start()

            @pl.when((pair == 1) & (g > 1))
            def _():
                reduce_a(g - 2)

            @pl.when((pair == 1) & (g > 2))
            def _():
                reduce_c(g - 3)

            attend_pair(g, pair)

        @pl.when(g > 1)
        def _():
            reduce_b(g - 2)

        @pl.when(g > 0)
        def _():
            reduce_core(g - 1)

    last = GROUPS - 1
    for i, ref in enumerate((dk_ref, dv_ref)):
        ref[last, 0:128, :] = edge_ref[last % 2, 0, i].astype(BF16)
        ref[last, 896:1024, :] = edge_ref[last % 2, 1, i].astype(BF16)
    for t in range(3):
        terms(last, (t,), t > 0)
        swap(last, t).start()
    for r in range(2):
        rows = slice(r * 256, (r + 1) * 256)
        for n in range(4):
            cols = slice(n * 256, (n + 1) * 256)
            total = None
            for g in range(GROUPS):
                part = nt(dq_ref[g, rows], w_ref[0, g, cols])
                total = part if total is None else total + part
            mg_ref[rows, cols] = total.astype(BF16)
    pltpu.make_async_copy(mg_ref, mg_hbm, out_sem.at[0]).start()

    def grid_grads(n):
        cols = slice(n * 256, (n + 1) * 256)
        for r in range(4):
            rows = slice(r * 256, (r + 1) * 256)
            total = None
            for g in range(GROUPS):
                for i, ref in enumerate((dk_ref, dv_ref)):
                    part = nt(ref[g, rows], w_ref[1 + i, g, cols])
                    total = part if total is None else total + part
            gg_ref[rows, cols] = total.astype(BF16)
        grid_out(n).start()

    def grid_out(n):
        return pltpu.make_async_copy(
            gg_ref.at[:, n * 256:(n + 1) * 256], gg_hbm.at[:, n * 256:(n + 1) * 256], out_sem.at[1 + n]
        )

    reduce_core(last, (0,))
    reduce_core(last, (1,))
    merge(last)
    reduce_core(last, (2,))
    reduce_a(last - 1)
    grid_grads(0)
    grid_grads(1)
    reduce_c(last - 2)
    reduce_b(last - 1)
    grid_grads(2)
    grid_grads(3)
    reduce_a(last)
    reduce_c(last - 1)
    reduce_b(last)
    reduce_c(last)
    copy = pltpu.make_async_copy(wg_ref, wg_hbm, out_sem.at[5])
    copy.start()
    copy.wait()
    pltpu.make_async_copy(mg_ref, mg_hbm, out_sem.at[0]).wait()
    for n in range(4):
        grid_out(n).wait()


def hand_out(gg, mg, wg, gg_out, mg_out, wg_out, gg_ref, mg_ref, wg_ref, sem):
    steps = []
    for src, held, dst, parts in ((gg, gg_ref, gg_out, 4), (mg, mg_ref, mg_out, 2), (wg, wg_ref, wg_out, 1)):
        rows = src.shape[0] // parts
        for part in range(parts):
            at = pl.ds(part * rows, rows)
            n = len(steps)
            steps.append((
                pltpu.make_async_copy(src.at[at], held.at[at], sem.at[0, n]),
                pltpu.make_async_copy(held.at[at], dst.at[at], sem.at[1, n]),
            ))
    for come, _ in steps:
        come.start()
    for come, go in steps:
        come.wait()
        go.start()
    for _, go in steps:
        go.wait()


def on_device(grid_feat, mesh_feat, mesh_adjoint, w_query, w_key, w_value, block_grid, block_mask):
    anywhere = pl.BlockSpec(memory_space=pl.ANY)
    dma = pltpu.SemaphoreType.DMA
    grid_grad, mesh_grad, w_grad = pl.pallas_call(
        kernel,
        in_specs=[pl.BlockSpec(memory_space=pltpu.SMEM)] + [anywhere] * 7,
        out_specs=[anywhere] * 3,
        out_shape=[
            jax.ShapeDtypeStruct((1024, D), BF16),
            jax.ShapeDtypeStruct((512, D), BF16),
            jax.ShapeDtypeStruct((8, 3 * D), F32),
        ],
        scratch_shapes=[
            pltpu.VMEM((1024, D), BF16),
            pltpu.VMEM((512, D), BF16),
            pltpu.VMEM((D, 1024), BF16),
            pltpu.VMEM((D, 512), BF16),
            pltpu.VMEM((3, GROUPS, D, W), BF16),
            pltpu.VMEM((16, 128, 128), jnp.int32),
            pltpu.VMEM((4, 512, 128), F32),
            pltpu.VMEM((GROUPS, 512, W), BF16),
            pltpu.VMEM((2, 512, W), BF16),
            pltpu.VMEM((2, 10, 128, W), BF16),
            pltpu.VMEM((2, 10, 128, W), BF16),
            pltpu.VMEM((GROUPS, 512, W), BF16),
            pltpu.VMEM((GROUPS, 1024, W), BF16),
            pltpu.VMEM((GROUPS, 1024, W), BF16),
            pltpu.VMEM((17, 128, 128), F32),
            pltpu.VMEM((17, 128, 128), F32),
            pltpu.VMEM((2, 2, 2, 128, W), F32),
            pltpu.VMEM((GROUPS, 2, 2, 128, W), BF16),
            pltpu.VMEM((GROUPS, 2, 2, 128, W), BF16),
            pltpu.VMEM((GROUPS, 2, 2, 128, W), BF16),
            pltpu.VMEM((GROUPS, 2, 2, 128, W), BF16),
            pltpu.VMEM((GROUPS, 2, 3, 512, W), BF16),
            pltpu.VMEM((GROUPS, 3, 512, W), BF16),
            pltpu.VMEM((GROUPS, 3, 512, W), BF16),
            pltpu.VMEM((GROUPS, 3, 3, 128, W), BF16),
            pltpu.VMEM((GROUPS, 3, 128, W), BF16),
            pltpu.VMEM((GROUPS, 3, 3, 32, W), BF16),
            pltpu.VMEM((GROUPS, 3, 32, W), F32),
            pltpu.VMEM((GROUPS, 3, 3, 8, W), F32),
            pltpu.VMEM((8, 3 * D), F32),
            pltpu.VMEM((1024, D), BF16),
            pltpu.VMEM((512, D), BF16),
            pltpu.VMEM((2, 128, D), BF16),
            pltpu.VMEM((D, 256), BF16),
            dma((2, 2)),
            pltpu.SMEM((16,), jnp.int32),
            pltpu.SMEM((40,), jnp.int32),
            dma((7,)),
            dma((GROUPS, 3)),
            dma((6,)),
            dma((2, GROUPS)),
            dma((2, GROUPS, 2)),
            dma((2, GROUPS, 2)),
            dma((2, GROUPS, 3)),
            dma((2, GROUPS)),
            dma((2, GROUPS)),
            dma((2, GROUPS)),
        ],
        compiler_params=pltpu.CompilerParams(
            collective_id=0, has_side_effects=True, vmem_limit_bytes=62 << 20
        ),
        cost_estimate=pl.CostEstimate(flops=20 * 2**30, bytes_accessed=20 << 20, transcendentals=4 << 20),
    )(block_grid, grid_feat[0], mesh_feat[0], mesh_adjoint[0], w_query, w_key, w_value, block_mask)
    results = (grid_grad, mesh_grad, w_grad)
    grid_grad, mesh_grad, w_grad = pl.pallas_call(
        hand_out,
        in_specs=[anywhere] * 3,
        out_specs=[anywhere] * 3,
        out_shape=[jax.ShapeDtypeStruct(r.shape, r.dtype) for r in results],
        scratch_shapes=[pltpu.VMEM(r.shape, r.dtype) for r in results] + [dma((2, 7))],
    )(*results)
    return (grid_grad[None], mesh_grad[None], w_grad)


def solution(mesh):
    placed = (
        P("sec", "space", None),
        P("sec", "space", None),
        P("sec", "space", None),
        P(),
        P(),
        P(),
        P("space"),
        P("space", None, None),
    )
    return jax.shard_map(
        on_device,
        mesh=mesh,
        in_specs=placed,
        out_specs=(P("sec", "space", None), P("sec", "space", None), P(("sec", "space"), None)),
        check_vma=False,
    )
```
